32 devices in a mesh: seq: 4 (over y, core), chan: 2 (over x), dp: 4 (over z).
Axes of the slice: x: 2, y: 2, z: 4, core: 2. Of those that a mesh axis runs over, the one named last changes fastest.
Arguments:
- inputs: bfloat16 [8, 4096, 512], P('dp', 'chan', 'seq'), may hold values from -0.0234375 to 0.0234375
- output_grad: bfloat16 [8, 4096, 512], P('dp', 'chan', 'seq'), may hold values from -6 to 6
- filters: bfloat16 [256, 512], P('chan', 'seq'), may hold values from -0.25 to 0.25
Outputs:
- input_grad: bfloat16 [8, 4096, 512], P('dp', 'chan', 'seq')
- filter_grad: float32 [256, 512], P('chan', 'seq')
The draws below stay inside these ranges and needn't reach their ends.
All inputs are finite; a program needn't handle non-finite values.
Results may differ from the reference program's by a relative error of at most 0.001.
Values may be sent and summed in bfloat16 or wider, within the bound.
No kernel may reach another device: no remote copies, remote signals or barrier semaphores. Data moves between devices by JAX's collectives and lax.ppermute only.
A program may use at most 128 MiB of HBM per device.

```python
import jax
import jax.numpy as jnp
from jax import lax

CHANNELS = 4096
GROUP_SIZE = 16
GROUPS = 256
LENGTH = 512
BATCH = 8


def levels(key, shape, shards, low, largest):
    factor_of, own = 1.0, jax.random.fold_in(key, 6)
    for position, blocks in shards:
        draws = jnp.exp(jax.random.uniform(jax.random.fold_in(own, position), (blocks,), jnp.float32, low / len(shards), largest / len(shards)))
        factor_of = factor_of * jnp.repeat(draws, shape[position] // blocks).reshape([-1 if axis == position else 1 for axis in range(len(shape))])
    return factor_of


def gaussian(own_key, dims, width, limit, pieces=(), kind=jnp.bfloat16):
    level = levels(own_key, dims, pieces, -0.22, 0.18) if pieces else 1.0
    values = jax.random.normal(own_key, dims, jnp.float32) * width * level
    return jnp.minimum(jnp.maximum(values, -limit), limit).astype(kind)


def setup_inputs(seed: int = 0) -> dict:
    splits = jax.random.split(jax.random.key(seed), 4)
    return {
        "inputs": gaussian(splits[0], (BATCH, CHANNELS, LENGTH), (BATCH * GROUP_SIZE * LENGTH) ** -0.5, 0.0234375, ((0, 4), (1, 2), (2, 4))),
        "output_grad": gaussian(splits[1], (BATCH, CHANNELS, LENGTH), 1.0, 6.0, ((0, 4), (1, 2), (2, 4))),
        "filters": gaussian(splits[2], (GROUPS, LENGTH), LENGTH ** -0.5, 0.25, ((0, 2), (1, 4))),
    }


def diagonal_sums(products, positions):
    leading = products.shape[0]
    flattened = products.reshape(leading, 2 * positions * positions)[:, : positions * (2 * positions - 1)]
    return jnp.sum(flattened.reshape(leading, positions, 2 * positions - 1), axis=1)


def reference(inputs, output_grad, filters):
    sequences, channels, length = inputs.shape
    group_count = channels // GROUP_SIZE
    grouped_inputs = jnp.transpose(inputs.reshape(sequences, group_count, GROUP_SIZE, length), (1, 0, 2, 3))
    grouped_grads = jnp.transpose(output_grad.reshape(sequences, group_count, GROUP_SIZE, length), (1, 0, 2, 3))
    rows_index = jnp.arange(length, dtype=jnp.int32)

    def one_group(arguments):
        taps, group_inputs, group_grads = arguments
        padded = jnp.pad(taps.astype(jnp.float32), (length, 0))
        index = (rows_index[None, :] - rows_index[:, None] + length).astype(jnp.int32)
        matrix = padded[index]
        input_part = jnp.einsum('bct,st->bcs', group_grads.astype(jnp.float32), matrix)
        flipped = group_inputs.astype(jnp.float32)[:, :, ::-1]
        products = jnp.einsum('bcs,bct->st', flipped, group_grads.astype(jnp.float32))
        products = jnp.pad(products, ((0, 0), (0, length)))
        lag_part = diagonal_sums(products[None], length)[0, length - 1:]
        return input_part, lag_part

    input_parts, lag_parts = lax.map(one_group, (filters, grouped_inputs, grouped_grads))
    input_grad = jnp.transpose(input_parts, (1, 0, 2, 3)).reshape(sequences, channels, length).astype(jnp.bfloat16)
    return input_grad, lag_parts
```

```python
import functools

import jax
import jax.numpy as jnp
from jax import lax
from jax.experimental import pallas as pl
from jax.experimental.pallas import tpu as pltpu
from jax.sharding import PartitionSpec as P

GROUP_SIZE = 16
CORES = 2
VMEM_BYTES = 40 << 20


def pick(condition, first, second):
    return jnp.where(condition, first, second)


def group_rows(ref, index):
    sequences, _, positions = ref.shape
    start = pl.multiple_of(index * GROUP_SIZE, GROUP_SIZE)
    return ref[:, pl.ds(start, GROUP_SIZE), :].reshape(sequences * GROUP_SIZE, positions)


def input_grad_kernel(chips, place, *refs):
    lag_blocks = CORES * chips
    filter_refs, refs = refs[:lag_blocks], refs[lag_blocks:]
    own_grad, peer_grad, refs = refs[0], refs[1], refs[2:]
    round_refs, (mine, theirs, taps) = refs[: 2 * (chips - 1)], refs[2 * (chips - 1) :]
    first_core = place[0] == 0
    chip = place[1]
    sequences, channels, positions = own_grad.shape
    rows = sequences * GROUP_SIZE
    width = lag_blocks * positions
    taps[...] = jnp.concatenate([ref[...] for ref in filter_refs], axis=1).astype(jnp.float32)
    row = lax.broadcasted_iota(jnp.int32, (positions, width), 0)
    column = lax.broadcasted_iota(jnp.int32, (positions, width), 1)
    causal = column >= row

    def one_group(index, carry):
        strip = jnp.broadcast_to(taps[pl.ds(index, 1), :], (positions, width))
        strip = pltpu.roll(strip, 0, 1, stride=1, stride_axis=0)
        strip = jnp.where(causal, strip, 0.0).astype(jnp.bfloat16)
        zeros = jnp.zeros((rows, positions), jnp.bfloat16)
        own, peer = group_rows(own_grad, index), group_rows(peer_grad, index)
        blocks = [pick(first_core, own, peer), pick(first_core, peer, own)]
        for distance in range(1, chips):
            received = [group_rows(ref, index) for ref in round_refs[2 * distance - 2 : 2 * distance]]
            lower = chip + distance < chips
            blocks.append(pick(lower, pick(first_core, *received), zeros))
            blocks.append(pick(lower, pick(first_core, *received[::-1]), zeros))
        grads = jnp.concatenate(
            [jnp.concatenate(blocks, axis=1), jnp.concatenate(blocks[1:] + [zeros], axis=1)], axis=0
        )
        sums = lax.dot_general(
            grads, strip, (((1,), (1,)), ((), ())), preferred_element_type=jnp.float32
        ).astype(jnp.bfloat16)
        start = pl.multiple_of(index * GROUP_SIZE, GROUP_SIZE)
        shape = (sequences, GROUP_SIZE, positions)
        early, late = sums[:rows], sums[rows:]
        mine[:, pl.ds(start, GROUP_SIZE), :] = pick(first_core, early, late).reshape(shape)
        theirs[:, pl.ds(start, GROUP_SIZE), :] = pick(first_core, late, early).reshape(shape)
        return carry

    lax.fori_loop(0, channels // GROUP_SIZE, one_group, 0, unroll=4)


def reversal(positions):
    row = lax.broadcasted_iota(jnp.int32, (positions, positions), 0)
    column = lax.broadcasted_iota(jnp.int32, (positions, positions), 1)
    return (row + column == positions - 1).astype(jnp.float32).astype(jnp.bfloat16)


def lag_sums(values, grads, flip, keep):
    positions, width = flip.shape[0], grads.shape[1]
    flipped = jnp.dot(values, flip, preferred_element_type=jnp.float32).astype(jnp.bfloat16)
    products = lax.dot_general(
        flipped, grads, (((0,), (0,)), ((), ())), preferred_element_type=jnp.float32
    )
    if keep is not None:
        products = jnp.where(keep, products, 0.0)
    products = pltpu.roll(products, width - positions + 1, 1, stride=1, stride_axis=0)
    return jnp.sum(products, axis=0, keepdims=True)


def own_lags_kernel(place, own_input, peer_input, own_grad, peer_grad, out):
    first_core = place[0] == 0
    sequences, channels, positions = own_input.shape
    rows, width = sequences * GROUP_SIZE, CORES * positions
    flip = reversal(positions)
    row = lax.broadcasted_iota(jnp.int32, (positions, width), 0)
    column = lax.broadcasted_iota(jnp.int32, (positions, width), 1)
    keep = column + row >= positions - 1

    def one_group(index, carry):
        own, peer = group_rows(own_input, index), group_rows(peer_input, index)
        values = jnp.concatenate([pick(first_core, own, peer), pick(first_core, peer, own)], axis=0)
        own, peer = group_rows(own_grad, index), group_rows(peer_grad, index)
        early, late = pick(first_core, own, peer), pick(first_core, peer, own)
        grads = jnp.concatenate(
            [
                jnp.concatenate([early, late], axis=1),
                jnp.concatenate([late, jnp.zeros((rows, positions), jnp.bfloat16)], axis=1),
            ],
            axis=0,
        )
        out[pl.ds(index, 1), :] = lag_sums(values, grads, flip, keep)
        return carry

    lax.fori_loop(0, channels // GROUP_SIZE, one_group, 0, unroll=4)


def round_lags_kernel(
    chips, distance, place, own_input, peer_input, own_grad, peer_grad, own_got, peer_got, running, out
):
    first_core = place[0] == 0
    lower = place[1] + distance < chips
    sequences, channels, positions = own_input.shape
    rows = sequences * GROUP_SIZE
    flip = reversal(positions)
    out[...] = running[...]
    if 2 * distance == chips:
        first_lag = (2 * distance - 2) * positions
    else:
        first_lag = pl.multiple_of(
            jnp.where(lower, 2 * distance - 2, 2 * (chips - distance) - 2) * positions, positions
        )

    def one_group(index, carry):
        got = group_rows(own_got, index), group_rows(peer_got, index)
        inputs = group_rows(own_input, index), group_rows(peer_input, index)
        grads = group_rows(own_grad, index), group_rows(peer_grad, index)
        left = [pick(lower, a, b) for a, b in zip(inputs, got)]
        right = [pick(lower, b, a) for a, b in zip(grads, got)]
        values = jnp.concatenate([pick(first_core, *left), pick(first_core, *left[::-1])], axis=0)
        early, late = pick(first_core, *right), pick(first_core, *right[::-1])
        zeros = jnp.zeros((rows, positions), jnp.bfloat16)
        pairs = jnp.concatenate(
            [
                jnp.concatenate([zeros, zeros, early, late], axis=1),
                jnp.concatenate([zeros, early, late, zeros], axis=1),
            ],
            axis=0,
        )
        where = (pl.ds(index, 1), pl.ds(first_lag, 2 * CORES * positions))
        out[where] = out[where] + lag_sums(values, pairs, flip, None)
        return carry

    lax.fori_loop(0, channels // GROUP_SIZE, one_group, 0, unroll=4)


def per_device(inputs, output_grad, filters):
    sequences, channels, positions = inputs.shape
    shard_count = lax.axis_size("seq")
    chips = shard_count // CORES
    own_index = lax.axis_index("seq")
    chip, core = own_index // CORES, own_index % CORES
    place = jnp.stack([core, chip]).astype(jnp.int32)
    half = channels // CORES
    part = half // 2
    groups, part_groups = half // GROUP_SIZE, part // GROUP_SIZE
    length = shard_count * positions

    def swap_cores(value):
        return lax.ppermute(value, "seq", [(i, i ^ 1) for i in range(shard_count)])

    def half_of(value, which):
        return lax.dynamic_slice_in_dim(value, which * half, half, 1)

    def from_chip(value, distance, wrap):
        pairs = [
            (i, (i - distance * CORES) % shard_count)
            for i in range(shard_count)
            if wrap or i >= distance * CORES
        ]
        return lax.ppermute(value, "seq", pairs)

    grad_own, input_own = half_of(output_grad, core), half_of(inputs, core)
    grad_peer = swap_cores(half_of(output_grad, 1 - core))
    input_peer = swap_cores(half_of(inputs, 1 - core))

    rounds = range(1, chips)
    first, second = {}, {}
    for k in rounds:
        sends_grad = chip >= k
        first[k] = (
            from_chip(jnp.where(sends_grad, grad_own[:, :part], input_own[:, part:]), k, True),
            from_chip(jnp.where(sends_grad, grad_peer[:, :part], input_peer[:, part:]), k, True),
        )
    for k in rounds:
        second[k] = (
            from_chip(grad_own[:, part:], k, False),
            from_chip(grad_peer[:, part:], k, False),
        )

    taps = jnp.stack([filters, swap_cores(filters)])
    taps = jnp.stack([taps] + [from_chip(taps, k, True) for k in rounds])

    step = min(16, part_groups)
    block = (sequences, step * GROUP_SIZE, positions)
    steps = part_groups // step

    def whole_spec(part_of=None):
        if part_of is None:
            return pl.BlockSpec(block, lambda i, place: (0, place[0] * 2 * steps + i, 0))
        return pl.BlockSpec(block, lambda i, place: (0, (place[0] * 2 + part_of(place)) * steps + i, 0))

    def half_spec(part_of=None):
        if part_of is None:
            return pl.BlockSpec(block, lambda i, place: (0, i, 0))
        return pl.BlockSpec(block, lambda i, place: (0, part_of(place) * steps + i, 0))

    part_spec = pl.BlockSpec(block, lambda i, place: (0, i, 0))
    params = pltpu.CompilerParams(vmem_limit_bytes=VMEM_BYTES)

    lags = pl.pallas_call(
        own_lags_kernel,
        grid_spec=pltpu.PrefetchScalarGridSpec(
            num_scalar_prefetch=1,
            grid=(2 * steps,),
            in_specs=[whole_spec(), half_spec(), whole_spec(), half_spec()],
            out_specs=pl.BlockSpec((step, CORES * positions), lambda i, place: (i, 0)),
        ),
        out_shape=jax.ShapeDtypeStruct((groups, CORES * positions), jnp.float32),
        compiler_params=params,
    )(place, inputs, input_peer, output_grad, grad_peer)
    lags = jnp.pad(lags, ((0, 0), (0, length - CORES * positions)))

    for k in rounds:
        def part_of(place, k=k):
            return jnp.where(place[1] + k < chips, 0, 1)

        lag_spec = pl.BlockSpec((step, length), lambda i, place, part_of=part_of: (part_of(place) * steps + i, 0))
        lags = pl.pallas_call(
            functools.partial(round_lags_kernel, chips, k),
            grid_spec=pltpu.PrefetchScalarGridSpec(
                num_scalar_prefetch=1,
                grid=(steps,),
                in_specs=[
                    whole_spec(part_of), half_spec(part_of), whole_spec(part_of), half_spec(part_of),
                    part_spec, part_spec, lag_spec,
                ],
                out_specs=lag_spec,
            ),
            out_shape=jax.ShapeDtypeStruct((groups, length), jnp.float32),
            input_output_aliases={7: 0},
            compiler_params=params,
        )(place, inputs, input_peer, output_grad, grad_peer, *first[k], lags)

    def input_part(which, received):
        def fixed(place):
            return which

        def filter_spec(block_index):
            def index(i, place):
                rotation = lax.rem(block_index // CORES - place[1] + chips, chips)
                other = jnp.where(place[0] == block_index % CORES, 0, 1)
                return (rotation, other, (place[0] * 2 + which) * steps + i, 0)

            return pl.BlockSpec((None, None, step, positions), index)

        arrays = [ref for k in rounds for ref in received[k]]
        return pl.pallas_call(
            functools.partial(input_grad_kernel, chips),
            grid_spec=pltpu.PrefetchScalarGridSpec(
                num_scalar_prefetch=1,
                grid=(steps,),
                in_specs=[filter_spec(q) for q in range(shard_count)]
                + [whole_spec(fixed), half_spec(fixed)]
                + [part_spec] * len(arrays),
                out_specs=[part_spec, part_spec],
                scratch_shapes=[pltpu.VMEM((step, length), jnp.float32)],
            ),
            out_shape=[jax.ShapeDtypeStruct((sequences, part, positions), jnp.bfloat16)] * 2,
            compiler_params=params,
        )(place, *([taps] * shard_count), output_grad, grad_peer, *arrays)

    parts = []
    for which, received in ((0, first), (1, second)):
        mine, theirs = input_part(which, received)
        parts.append((mine, swap_cores(theirs)))
    mine = jnp.concatenate([p[0] for p in parts], axis=1)
    got = jnp.concatenate([p[1] for p in parts], axis=1)
    input_grad = jnp.where(
        core == 0, jnp.concatenate([mine, got], axis=1), jnp.concatenate([got, mine], axis=1)
    )

    def chip_lags(which):
        return lax.dynamic_slice_in_dim(lags, which * CORES * positions, CORES * positions, 1)

    sums = chip_lags(chip)
    for k in rounds:
        sums = sums + from_chip(chip_lags((chip - k) % chips), k, True)
    keep = lax.dynamic_slice_in_dim(sums, core * positions, positions, 1)
    got = swap_cores(lax.dynamic_slice_in_dim(sums, (1 - core) * positions, positions, 1))
    own = jnp.where(core == 0, jnp.concatenate([keep, got], axis=0), jnp.concatenate([got, keep], axis=0))
    copies = lax.axis_size("dp")
    terms = [own]
    for k in range(1, copies):
        terms.append(lax.ppermute(own, "dp", [(i, i ^ k) for i in range(copies)]))
    while len(terms) > 1:
        terms = [a + b for a, b in zip(terms[::2], terms[1::2])]
    filter_grad = terms[0]
    return (input_grad, filter_grad)


def solution(mesh):
    in_specs = (P("dp", "chan", "seq"), P("dp", "chan", "seq"), P("chan", "seq"))
    out_specs = (P("dp", "chan", "seq"), P("chan", "seq"))
    return jax.shard_map(
        per_device, mesh=mesh, in_specs=in_specs, out_specs=out_specs, check_vma=False
    )
```

```python
import functools

import jax
import jax.numpy as jnp
from jax import lax
from jax.experimental import pallas as pl
from jax.experimental.pallas import tpu as pltpu
from jax.sharding import PartitionSpec as P

GROUP_SIZE = 16
CORES = 2
VMEM_BYTES = 40 << 20
UNROLL = 16


def pick(condition, first, second):
    return jnp.where(condition, first, second)


def group_rows(ref, index):
    sequences, _, positions = ref.shape
    start = pl.multiple_of(index * GROUP_SIZE, GROUP_SIZE)
    return ref[:, pl.ds(start, GROUP_SIZE), :].reshape(sequences * GROUP_SIZE, positions)


def input_grad_kernel(chips, place, *refs):
    lag_blocks = CORES * chips
    filter_refs, refs = refs[:lag_blocks], refs[lag_blocks:]
    own_grad, peer_grad, refs = refs[0], refs[1], refs[2:]
    round_refs, (mine, theirs, taps) = refs[: 2 * (chips - 1)], refs[2 * (chips - 1) :]
    first_core = place[0] == 0
    chip = place[1]
    sequences, channels, positions = own_grad.shape
    rows = sequences * GROUP_SIZE
    width = lag_blocks * positions
    taps[...] = jnp.concatenate([ref[...] for ref in filter_refs], axis=1).astype(jnp.float32)
    row = lax.broadcasted_iota(jnp.int32, (positions, width), 0)
    column = lax.broadcasted_iota(jnp.int32, (positions, width), 1)
    causal = column >= row

    def one_group(index, carry):
        strip = jnp.broadcast_to(taps[pl.ds(index, 1), :], (positions, width))
        strip = pltpu.roll(strip, 0, 1, stride=1, stride_axis=0)
        strip = jnp.where(causal, strip, 0.0).astype(jnp.bfloat16)
        zeros = jnp.zeros((rows, positions), jnp.bfloat16)
        own, peer = group_rows(own_grad, index), group_rows(peer_grad, index)
        blocks = [pick(first_core, own, peer), pick(first_core, peer, own)]
        for distance in range(1, chips):
            received = [group_rows(ref, index) for ref in round_refs[2 * distance - 2 : 2 * distance]]
            lower = chip + distance < chips
            blocks.append(pick(lower, pick(first_core, *received), zeros))
            blocks.append(pick(lower, pick(first_core, *received[::-1]), zeros))
        grads = jnp.concatenate(
            [jnp.concatenate(blocks, axis=1), jnp.concatenate(blocks[1:] + [zeros], axis=1)], axis=0
        )
        sums = lax.dot_general(
            grads, strip, (((1,), (1,)), ((), ())), preferred_element_type=jnp.float32
        ).astype(jnp.bfloat16)
        start = pl.multiple_of(index * GROUP_SIZE, GROUP_SIZE)
        shape = (sequences, GROUP_SIZE, positions)
        early, late = sums[:rows], sums[rows:]
        mine[:, pl.ds(start, GROUP_SIZE), :] = pick(first_core, early, late).reshape(shape)
        theirs[:, pl.ds(start, GROUP_SIZE), :] = pick(first_core, late, early).reshape(shape)
        return carry

    lax.fori_loop(0, channels // GROUP_SIZE, one_group, 0, unroll=UNROLL)


def reversal(positions):
    row = lax.broadcasted_iota(jnp.int32, (positions, positions), 0)
    column = lax.broadcasted_iota(jnp.int32, (positions, positions), 1)
    return (row + column == positions - 1).astype(jnp.float32).astype(jnp.bfloat16)


def flip_rows(out, core, values, flip):
    sequences, channels, positions = values.shape
    flat = values.reshape(sequences * channels, positions)
    flat = jnp.dot(flat, flip, preferred_element_type=jnp.float32).astype(jnp.bfloat16)
    out[core] = flat.reshape(sequences, channels, positions)


def lag_sums(flipped, grads, keep, lead):
    products = lax.dot_general(
        flipped, grads, (((0,), (0,)), ((), ())), preferred_element_type=jnp.float32
    )
    positions = products.shape[0]
    if keep is not None:
        products = jnp.where(keep, products, 0.0)
    if lead:
        products = jnp.concatenate([jnp.zeros((positions, lead), jnp.float32), products], axis=1)
    products = pltpu.roll(products, products.shape[1] - positions + 1, 1, stride=1, stride_axis=0)
    return jnp.sum(products, axis=0, keepdims=True)


def own_lags_kernel(place, own_input, peer_input, own_grad, peer_grad, out, flipped):
    first_core = place[0] == 0
    sequences, channels, positions = own_input.shape
    rows, width = sequences * GROUP_SIZE, CORES * positions
    flip = reversal(positions)
    own, peer = own_input[...], peer_input[...]
    flip_rows(flipped, 0, pick(first_core, own, peer), flip)
    flip_rows(flipped, 1, pick(first_core, peer, own), flip)
    row = lax.broadcasted_iota(jnp.int32, (positions, width), 0)
    column = lax.broadcasted_iota(jnp.int32, (positions, width), 1)
    keep = column + row >= positions - 1

    def one_group(index, carry):
        values = jnp.concatenate([group_rows(flipped.at[core], index) for core in range(CORES)], axis=0)
        own, peer = group_rows(own_grad, index), group_rows(peer_grad, index)
        early, late = pick(first_core, own, peer), pick(first_core, peer, own)
        zeros = jnp.zeros((rows, positions), jnp.bfloat16)
        grads = jnp.concatenate(
            [jnp.concatenate([early, late], axis=1), jnp.concatenate([late, zeros], axis=1)], axis=0
        )
        out[pl.ds(index, 1), :] = lag_sums(values, grads, keep, 0)
        return carry

    lax.fori_loop(0, channels // GROUP_SIZE, one_group, 0, unroll=UNROLL)


def round_lags_kernel(
    chips,
    distance,
    place,
    own_input,
    peer_input,
    own_grad,
    peer_grad,
    own_got,
    peer_got,
    running,
    out,
    flipped,
):
    first_core = place[0] == 0
    lower = place[1] + distance < chips
    sequences, channels, positions = own_input.shape
    rows = sequences * GROUP_SIZE
    flip = reversal(positions)
    own, peer = (
        pick(lower, own_input[...], own_got[...]),
        pick(lower, peer_input[...], peer_got[...]),
    )
    flip_rows(flipped, 0, pick(first_core, own, peer), flip)
    flip_rows(flipped, 1, pick(first_core, peer, own), flip)
    out[...] = running[...]
    if 2 * distance == chips:
        first_lag = (2 * distance - 2) * positions
    else:
        first_lag = pl.multiple_of(
            jnp.where(lower, 2 * distance - 2, 2 * (chips - distance) - 2) * positions, positions
        )

    def one_group(index, carry):
        got = group_rows(own_got, index), group_rows(peer_got, index)
        grads = group_rows(own_grad, index), group_rows(peer_grad, index)
        right = [pick(lower, b, a) for a, b in zip(grads, got)]
        values = jnp.concatenate([group_rows(flipped.at[core], index) for core in range(CORES)], axis=0)
        early, late = pick(first_core, *right), pick(first_core, *right[::-1])
        zeros = jnp.zeros((rows, positions), jnp.bfloat16)
        pairs = jnp.concatenate(
            [
                jnp.concatenate([zeros, early, late], axis=1),
                jnp.concatenate([early, late, zeros], axis=1),
            ],
            axis=0,
        )
        where = (pl.ds(index, 1), pl.ds(first_lag, 2 * CORES * positions))
        out[where] = out[where] + lag_sums(values, pairs, None, positions)
        return carry

    lax.fori_loop(0, channels // GROUP_SIZE, one_group, 0, unroll=UNROLL)


def per_device(inputs, output_grad, filters):
    sequences, channels, positions = inputs.shape
    shard_count = lax.axis_size("seq")
    chips = shard_count // CORES
    own_index = lax.axis_index("seq")
    chip, core = own_index // CORES, own_index % CORES
    place = jnp.stack([core, chip]).astype(jnp.int32)
    half = channels // CORES
    part = half // 2
    groups, part_groups = half // GROUP_SIZE, part // GROUP_SIZE
    length = shard_count * positions

    def swap_cores(value):
        return lax.ppermute(value, "seq", [(i, i ^ 1) for i in range(shard_count)])

    def half_of(value, which):
        return lax.dynamic_slice_in_dim(value, which * half, half, 1)

    def from_chip(value, distance, wrap):
        pairs = [
            (i, (i - distance * CORES) % shard_count)
            for i in range(shard_count)
            if wrap or i >= distance * CORES
        ]
        return lax.ppermute(value, "seq", pairs)

    grad_own, input_own = half_of(output_grad, core), half_of(inputs, core)
    grad_peer = swap_cores(half_of(output_grad, 1 - core))
    input_peer = swap_cores(half_of(inputs, 1 - core))

    rounds = range(1, chips)
    first, second = {}, {}
    for k in rounds:
        sends_grad = chip >= k
        first[k] = (
            from_chip(jnp.where(sends_grad, grad_own[:, :part], input_own[:, part:]), k, True),
            from_chip(jnp.where(sends_grad, grad_peer[:, :part], input_peer[:, part:]), k, True),
        )
    for k in rounds:
        second[k] = (
            from_chip(grad_own[:, part:], k, False),
            from_chip(grad_peer[:, part:], k, False),
        )

    taps = jnp.stack([filters, swap_cores(filters)])
    taps = jnp.stack([taps] + [from_chip(taps, k, True) for k in rounds])

    step = min(16, part_groups)
    block = (sequences, step * GROUP_SIZE, positions)
    steps = part_groups // step

    def whole_spec(part_of=None):
        if part_of is None:
            return pl.BlockSpec(block, lambda i, place: (0, place[0] * 2 * steps + i, 0))
        return pl.BlockSpec(block, lambda i, place: (0, (place[0] * 2 + part_of(place)) * steps + i, 0))

    def half_spec(part_of=None):
        if part_of is None:
            return pl.BlockSpec(block, lambda i, place: (0, i, 0))
        return pl.BlockSpec(block, lambda i, place: (0, part_of(place) * steps + i, 0))

    part_spec = pl.BlockSpec(block, lambda i, place: (0, i, 0))
    params = pltpu.CompilerParams(vmem_limit_bytes=VMEM_BYTES)
    flip_scratch = [pltpu.VMEM((CORES,) + block, jnp.bfloat16)]
    rows = sequences * GROUP_SIZE

    def cost(group_count, depth, width, arrays):
        return pl.CostEstimate(
            flops=2 * group_count * depth * positions * width,
            bytes_accessed=arrays * group_count * rows * positions * 2,
            transcendentals=0,
        )

    lags = pl.pallas_call(
        own_lags_kernel,
        grid_spec=pltpu.PrefetchScalarGridSpec(
            num_scalar_prefetch=1,
            grid=(2 * steps,),
            in_specs=[whole_spec(), half_spec(), whole_spec(), half_spec()],
            out_specs=pl.BlockSpec((step, CORES * positions), lambda i, place: (i, 0)),
            scratch_shapes=flip_scratch,
        ),
        out_shape=jax.ShapeDtypeStruct((groups, CORES * positions), jnp.float32),
        cost_estimate=cost(groups, CORES * rows, CORES * positions, 4),
        compiler_params=params,
    )(place, inputs, input_peer, output_grad, grad_peer)
    lags = jnp.pad(lags, ((0, 0), (0, length - CORES * positions)))

    for k in rounds:
        def part_of(place, k=k):
            return jnp.where(place[1] + k < chips, 0, 1)

        lag_spec = pl.BlockSpec((step, length), lambda i, place, part_of=part_of: (part_of(place) * steps + i, 0))
        lags = pl.pallas_call(
            functools.partial(round_lags_kernel, chips, k),
            grid_spec=pltpu.PrefetchScalarGridSpec(
                num_scalar_prefetch=1,
                grid=(steps,),
                in_specs=[
                    whole_spec(part_of), half_spec(part_of), whole_spec(part_of), half_spec(part_of),
                    part_spec, part_spec, lag_spec,
                ],
                out_specs=lag_spec,
                scratch_shapes=flip_scratch,
            ),
            out_shape=jax.ShapeDtypeStruct((groups, length), jnp.float32),
            input_output_aliases={7: 0},
            cost_estimate=cost(part_groups, CORES * rows, 3 * positions, 6),
            compiler_params=params,
        )(place, inputs, input_peer, output_grad, grad_peer, *first[k], lags)

    def input_part(which, received):
        def fixed(place):
            return which

        def filter_spec(block_index):
            def index(i, place):
                rotation = lax.rem(block_index // CORES - place[1] + chips, chips)
                other = jnp.where(place[0] == block_index % CORES, 0, 1)
                return (rotation, other, (place[0] * 2 + which) * steps + i, 0)

            return pl.BlockSpec((None, None, step, positions), index)

        arrays = [ref for k in rounds for ref in received[k]]
        return pl.pallas_call(
            functools.partial(input_grad_kernel, chips),
            grid_spec=pltpu.PrefetchScalarGridSpec(
                num_scalar_prefetch=1,
                grid=(steps,),
                in_specs=[filter_spec(q) for q in range(shard_count)]
                + [whole_spec(fixed), half_spec(fixed)]
                + [part_spec] * len(arrays),
                out_specs=[part_spec, part_spec],
                scratch_shapes=[pltpu.VMEM((step, length), jnp.float32)],
            ),
            out_shape=[jax.ShapeDtypeStruct((sequences, part, positions), jnp.bfloat16)] * 2,
            cost_estimate=cost(part_groups, CORES * rows, length, 4 + len(arrays)),
            compiler_params=params,
        )(place, *([taps] * shard_count), output_grad, grad_peer, *arrays)

    parts = []
    for which, received in ((0, first), (1, second)):
        mine, theirs = input_part(which, received)
        parts.append((mine, swap_cores(theirs)))
    mine = jnp.concatenate([p[0] for p in parts], axis=1)
    got = jnp.concatenate([p[1] for p in parts], axis=1)
    input_grad = jnp.where(
        core == 0, jnp.concatenate([mine, got], axis=1), jnp.concatenate([got, mine], axis=1)
    )

    def chip_lags(which):
        return lax.dynamic_slice_in_dim(lags, which * CORES * positions, CORES * positions, 1)

    sums = chip_lags(chip)
    for k in rounds:
        sums = sums + from_chip(chip_lags((chip - k) % chips), k, True)
    keep = lax.dynamic_slice_in_dim(sums, core * positions, positions, 1)
    got = swap_cores(lax.dynamic_slice_in_dim(sums, (1 - core) * positions, positions, 1))
    own = jnp.where(core == 0, jnp.concatenate([keep, got], axis=0), jnp.concatenate([got, keep], axis=0))
    copies = lax.axis_size("dp")
    terms = [own]
    for k in range(1, copies):
        terms.append(lax.ppermute(own, "dp", [(i, i ^ k) for i in range(copies)]))
    while len(terms) > 1:
        terms = [a + b for a, b in zip(terms[::2], terms[1::2])]
    filter_grad = terms[0]
    return (input_grad, filter_grad)


def solution(mesh):
    in_specs = (P("dp", "chan", "seq"), P("dp", "chan", "seq"), P("chan", "seq"))
    out_specs = (P("dp", "chan", "seq"), P("chan", "seq"))
    return jax.shard_map(
        per_device, mesh=mesh, in_specs=in_specs, out_specs=out_specs, check_vma=False
    )
```

```python
import functools

import jax
import jax.numpy as jnp
from jax import lax
from jax.experimental import pallas as pl
from jax.experimental.pallas import tpu as pltpu
from jax.sharding import PartitionSpec as P

GROUP_SIZE = 16
CORES = 2
VMEM_BYTES = 16 << 20
UNROLL = 16
OWN_WEIGHT = 100
EARLY = 12
C1 = True
C2 = True


def pick(condition, first, second):
    return jnp.where(condition, first, second)


def group_rows(ref, index, first_row=0):
    sequences, _, positions = ref.shape
    start = pl.multiple_of(first_row + index * GROUP_SIZE, GROUP_SIZE)
    return ref[:, pl.ds(start, GROUP_SIZE), :].reshape(sequences * GROUP_SIZE, positions)


def chunked(groups, body):
    count = max(size for size in range(1, UNROLL + 1) if groups % size == 0)

    def chunk(number, carry):
        body(number * count, count)
        return carry

    lax.fori_loop(0, groups // count, chunk, 0)


def input_grad_kernel(chips, which, offset, slot_rows, place, *refs):
    filter_refs, refs = refs[: CORES * chips], refs[CORES * chips :]
    own_grad, peer_grad, refs = refs[0], refs[1], refs[2:]
    round_refs, (mine, theirs, taps) = list(refs[:-3]), refs[-3:]
    core, chip = place[0], place[1]
    first_core = core == 0
    sequences, size, positions = mine.shape
    part = own_grad.shape[1] // CORES // 2
    if len(round_refs) < CORES * (chips - 1):
        round_refs = [
            ref.at[pl.ds(core_of * sequences, sequences)] for ref in round_refs for core_of in range(CORES)
        ]
    groups = size // GROUP_SIZE
    first_taps = which * (part // GROUP_SIZE) + offset
    rows = sequences * GROUP_SIZE
    width = CORES * chips * positions
    own_row = pl.multiple_of((core * 2 + which) * part + offset * GROUP_SIZE, GROUP_SIZE)
    all_groups = taps.shape[0]
    own_taps = pl.ds(pl.multiple_of(core * all_groups, all_groups), all_groups)
    holders = range(all_groups // slot_rows)
    for rotation in range(chips):
        start = lax.rem(chip + rotation, chips) * (CORES * positions)
        pair = filter_refs[CORES * rotation : CORES * (rotation + 1)]
        if rotation == 0:
            pair = [ref[own_taps, :] for ref in pair]
        else:
            pair = [
                jnp.concatenate([ref[holder, part : part + slot_rows, :] for holder in holders], axis=0)
                for ref in pair
            ]
        pair = jnp.concatenate([pick(first_core, *pair), pick(first_core, *pair[::-1])], axis=1)
        taps[:, pl.ds(pl.multiple_of(start, positions), CORES * positions)] = pair.astype(jnp.float32)
    row = lax.broadcasted_iota(jnp.int32, (positions, width), 0)
    column = lax.broadcasted_iota(jnp.int32, (positions, width), 1)
    causal = column >= row
    zeros = jnp.zeros((rows, positions), jnp.bfloat16)

    def one_group(index):
        strip = jnp.broadcast_to(taps[pl.ds(first_taps + index, 1), :], (positions, width))
        strip = pltpu.roll(strip, 0, 1, stride=1, stride_axis=0)
        strip = jnp.where(causal, strip, 0.0).astype(jnp.bfloat16)
        own, peer = group_rows(own_grad, index, own_row), group_rows(peer_grad, index, own_row)
        blocks = [pick(first_core, own, peer), pick(first_core, peer, own)]
        for distance in range(1, chips):
            received = [group_rows(ref, index) for ref in round_refs[2 * distance - 2 : 2 * distance]]
            lower = chip + distance < chips
            blocks.append(pick(lower, pick(first_core, *received), zeros))
            blocks.append(pick(lower, pick(first_core, *received[::-1]), zeros))
        grads = jnp.concatenate(
            [jnp.concatenate(blocks, axis=1), jnp.concatenate(blocks[1:] + [zeros], axis=1)], axis=0
        )
        sums = lax.dot_general(
            grads, strip, (((1,), (1,)), ((), ())), preferred_element_type=jnp.float32
        ).astype(jnp.bfloat16)
        start = pl.multiple_of(index * GROUP_SIZE, GROUP_SIZE)
        shape = (sequences, GROUP_SIZE, positions)
        early, late = sums[:rows], sums[rows:]
        mine[:, pl.ds(start, GROUP_SIZE), :] = pick(first_core, early, late).reshape(shape)
        theirs[:, pl.ds(start, GROUP_SIZE), :] = pick(first_core, late, early).reshape(shape)

    def body(first, count):
        for index in range(count):
            one_group(first + index)

    chunked(groups, body)


def reversal(positions):
    row = lax.broadcasted_iota(jnp.int32, (positions, positions), 0)
    column = lax.broadcasted_iota(jnp.int32, (positions, positions), 1)
    return (row + column == positions - 1).astype(jnp.float32).astype(jnp.bfloat16)


def flip_rows(out, core, values, flip):
    sequences, channels, positions = values.shape
    flat = values.reshape(sequences * channels, positions)
    flat = jnp.dot(flat, flip, preferred_element_type=jnp.float32).astype(jnp.bfloat16)
    out[core, :, :channels, :] = flat.reshape(sequences, channels, positions)


def lag_sums(flipped, grads, keep, lead):
    products = lax.dot_general(
        flipped, grads, (((0,), (0,)), ((), ())), preferred_element_type=jnp.float32
    )
    positions = products.shape[0]
    if keep is not None:
        products = jnp.where(keep, products, 0.0)
    if lead:
        products = jnp.concatenate([jnp.zeros((positions, lead), jnp.float32), products], axis=1)
    products = pltpu.roll(products, products.shape[1] - positions + 1, 1, stride=1, stride_axis=0)
    return jnp.sum(products, axis=0, keepdims=True)


def own_lags_kernel(place, own_input, peer_input, own_grad, peer_grad, out, flipped):
    first_core = place[0] == 0
    sequences, channels, positions = own_input.shape
    half = channels // CORES
    own_row = pl.multiple_of(place[0] * half, half)
    rows, width = sequences * GROUP_SIZE, CORES * positions
    flip = reversal(positions)
    row = lax.broadcasted_iota(jnp.int32, (positions, width), 0)
    column = lax.broadcasted_iota(jnp.int32, (positions, width), 1)
    keep = column + row >= positions - 1
    zeros = jnp.zeros((rows, positions), jnp.bfloat16)
    out[...] = jnp.zeros_like(out)

    def body(first, count):
        start = pl.multiple_of(own_row + first * GROUP_SIZE, GROUP_SIZE)
        own = own_input[:, pl.ds(start, count * GROUP_SIZE), :]
        peer = peer_input[:, pl.ds(start, count * GROUP_SIZE), :]
        flip_rows(flipped, 0, pick(first_core, own, peer), flip)
        flip_rows(flipped, 1, pick(first_core, peer, own), flip)
        for index in range(count):
            values = jnp.concatenate(
                [group_rows(flipped.at[core], index) for core in range(CORES)], axis=0
            )
            own = group_rows(own_grad, index, start)
            peer = group_rows(peer_grad, index, start)
            early, late = pick(first_core, own, peer), pick(first_core, peer, own)
            grads = jnp.concatenate(
                [jnp.concatenate([early, late], axis=1), jnp.concatenate([late, zeros], axis=1)], axis=0
            )
            out[pl.ds(first + index, 1), :width] = lag_sums(values, grads, keep, 0)

    chunked(half // GROUP_SIZE, body)


def round_lags_kernel(
    chips, distance, place, own_input, peer_input, own_grad, peer_grad, own_got, peer_got, running, out, flipped
):
    first_core = place[0] == 0
    lower = place[1] + distance < chips
    sequences, channels, positions = own_input.shape
    part = channels // CORES // 2
    rows = sequences * GROUP_SIZE
    flip = reversal(positions)
    part_row = pl.multiple_of((place[0] * 2 + jnp.where(lower, 0, 1)) * part, part)
    part_group = pl.multiple_of(jnp.where(lower, 0, part // GROUP_SIZE), part // GROUP_SIZE)
    if 2 * distance == chips:
        first_lag = (2 * distance - 2) * positions
    else:
        first_lag = pl.multiple_of(
            jnp.where(lower, 2 * distance - 2, 2 * (chips - distance) - 2) * positions, positions
        )
    zeros = jnp.zeros((rows, positions), jnp.bfloat16)
    out[...] = running[...]

    def body(first, count):
        start = pl.multiple_of(first * GROUP_SIZE, GROUP_SIZE)
        own_rows = pl.ds(pl.multiple_of(part_row + start, GROUP_SIZE), count * GROUP_SIZE)
        got_rows = pl.ds(start, count * GROUP_SIZE)
        own = pick(lower, own_input[:, own_rows, :], own_got[:, got_rows, :])
        peer = pick(lower, peer_input[:, own_rows, :], peer_got[:, got_rows, :])
        flip_rows(flipped, 0, pick(first_core, own, peer), flip)
        flip_rows(flipped, 1, pick(first_core, peer, own), flip)
        for index in range(count):
            got = group_rows(own_got, index, start), group_rows(peer_got, index, start)
            grads = (
                group_rows(own_grad, index, part_row + start),
                group_rows(peer_grad, index, part_row + start),
            )
            right = [pick(lower, b, a) for a, b in zip(grads, got)]
            values = jnp.concatenate(
                [group_rows(flipped.at[core], index) for core in range(CORES)], axis=0
            )
            early, late = pick(first_core, *right), pick(first_core, *right[::-1])
            pairs = jnp.concatenate(
                [
                    jnp.concatenate([zeros, early, late], axis=1),
                    jnp.concatenate([early, late, zeros], axis=1),
                ],
                axis=0,
            )
            where = (pl.ds(part_group + first + index, 1), pl.ds(first_lag, 2 * CORES * positions))
            out[where] = out[where] + lag_sums(values, pairs, None, positions)

    chunked(part // GROUP_SIZE, body)


def assemble_kernel(out_place, *refs):
    parts, out, sems = refs[:-2], refs[-2], refs[-1]
    half = out.shape[1] // CORES
    core = out_place[0]
    copies = []
    start = core * half
    for number, ref in enumerate(parts):
        if number == len(parts) // 2:
            start = (1 - core) * half
        rows = pl.ds(pl.multiple_of(start, GROUP_SIZE), ref.shape[1])
        copies.append(pltpu.make_async_copy(ref, out.at[:, rows, :], sems.at[number]))
        start = start + ref.shape[1]
    for copy in copies:
        copy.start()
    for copy in copies:
        copy.wait()


def parts_kernel(chips, slot_rows, inputs, output_grad, filters, *refs):
    count = CORES * (chips - 1)
    outs, stages, in_sems, out_sems = refs[:count], refs[count : 2 * count], refs[-2], refs[-1]
    sequences = inputs.shape[0]
    half = inputs.shape[1] // CORES
    part = half // 2
    groups = filters.shape[0] // CORES
    own_index = lax.axis_index("seq")
    chip, core = lax.div(own_index, CORES), lax.rem(own_index, CORES)

    def arrival(source, start, target, number):
        return pltpu.make_async_copy(
            source.at[:, pl.ds(pl.multiple_of(start, GROUP_SIZE), part), :],
            target.at[:, pl.ds(0, part), :],
            in_sems.at[number],
        )

    for number in range(count):
        distance, other = number // CORES + 1, number % CORES
        whose = core if other == 0 else 1 - core
        start = whose * half
        target = stages[number]
        for sequence in range(sequences):
            slot = sequence if slot_rows < groups else 0
            row = pl.multiple_of(whose * groups + slot * slot_rows, GROUP_SIZE)
            pltpu.make_async_copy(
                filters.at[pl.ds(row, slot_rows), :],
                target.at[sequence, pl.ds(part, slot_rows), :],
                in_sems.at[number],
            ).start()
        lax.cond(
            chip >= distance,
            lambda: arrival(output_grad, start, target, number).start(),
            lambda: arrival(inputs, start + part, target, number).start(),
        )
    for number in range(count):
        pltpu.make_async_copy(stages[number], stages[number], in_sems.at[number]).wait()
        pltpu.make_async_copy(stages[number], outs[number], out_sems.at[number]).start()
    for number in range(count):
        pltpu.make_async_copy(stages[number], outs[number], out_sems.at[number]).wait()


def second_kernel(own_grad, peer_grad, *refs):
    outs, sems = refs[:-1], refs[-1]
    sequences = own_grad.shape[0]
    half = own_grad.shape[1] // CORES
    core = lax.rem(lax.axis_index("seq"), CORES)
    start = core * half + half // 2
    copies = []
    for out in outs:
        for number, ref in enumerate((own_grad, peer_grad)):
            copies.append(
                pltpu.make_async_copy(
                    ref.at[:, pl.ds(pl.multiple_of(start, GROUP_SIZE), out.shape[1]), :],
                    out.at[pl.ds(number * sequences, sequences)],
                    sems.at[len(copies)],
                )
            )
        start = start + out.shape[1]
    for copy in copies:
        copy.start()
    for copy in copies:
        copy.wait()


def per_device(inputs, output_grad, filters):
    sequences, channels, positions = inputs.shape
    shard_count = lax.axis_size("seq")
    chips = shard_count // CORES
    own_index = lax.axis_index("seq")
    chip, core = own_index // CORES, own_index % CORES
    place = jnp.stack([core, chip]).astype(jnp.int32)
    half = channels // CORES
    part = half // 2
    groups = half // GROUP_SIZE
    slot_rows = groups // 2 if sequences == 2 and groups % (2 * GROUP_SIZE) == 0 else groups
    length = shard_count * positions
    rows = sequences * GROUP_SIZE
    rounds = range(1, chips)

    def swap_cores(value):
        return lax.ppermute(value, "seq", [(i, i ^ 1) for i in range(shard_count)])

    def from_chip(value, distance, wrap, other=0):
        pairs = [
            (i, (i - distance * CORES) % shard_count ^ other)
            for i in range(shard_count)
            if wrap or i >= distance * CORES
        ]
        return lax.ppermute(value, "seq", pairs)

    in_hbm = pl.BlockSpec(memory_space=pltpu.HBM)
    params = pltpu.CompilerParams(vmem_limit_bytes=VMEM_BYTES)

    filters_peer = swap_cores(filters)
    grad_peer, input_peer = swap_cores(output_grad), swap_cores(inputs)

    heights = [part + slot_rows] * (CORES * (chips - 1))
    outgoing = pl.pallas_call(
        functools.partial(parts_kernel, chips, slot_rows),
        in_specs=[in_hbm] * 3,
        out_specs=[in_hbm] * len(heights),
        out_shape=[jax.ShapeDtypeStruct((sequences, height, positions), inputs.dtype) for height in heights],
        scratch_shapes=[pltpu.VMEM((sequences, height, positions), inputs.dtype) for height in heights]
        + [pltpu.SemaphoreType.DMA((len(heights),))] * 2,
    )(inputs, output_grad, filters)

    first = {
        k: [from_chip(outgoing[CORES * (k - 1) + other], k, True, other) for other in range(CORES)]
        for k in rounds
    }

    in_smem, in_vmem = pl.BlockSpec(memory_space=pltpu.SMEM), pl.BlockSpec(memory_space=pltpu.VMEM)
    flip_scratch = pltpu.VMEM((CORES, sequences, UNROLL * GROUP_SIZE, positions), jnp.bfloat16)

    def vmem(value):
        return pltpu.with_memory_space_constraint(value, pltpu.VMEM)

    def cost(group_count, depth, width, arrays):
        return pl.CostEstimate(
            flops=2 * group_count * depth * positions * width,
            bytes_accessed=arrays * group_count * rows * positions * 2,
            transcendentals=0,
        )

    input_here, grad_here = vmem(inputs), vmem(output_grad)
    input_peer, grad_peer = vmem(input_peer), vmem(grad_peer)
    both = (input_here, input_peer, grad_here, grad_peer)
    part_groups = groups // 2
    early_groups = part_groups * EARLY // 32
    sizes = [early_groups, part_groups - early_groups]
    outgoing = pl.pallas_call(
        second_kernel,
        in_specs=[in_vmem] * 2,
        out_specs=[in_hbm] * len(sizes),
        out_shape=[
            jax.ShapeDtypeStruct((CORES * sequences, size * GROUP_SIZE, positions), inputs.dtype) for size in sizes
        ],
        scratch_shapes=[pltpu.SemaphoreType.DMA((CORES * len(sizes),))],
    )(grad_here, grad_peer)
    second = [{k: [from_chip(value, k, False)] for k in rounds} for value in outgoing]

    lags = pl.pallas_call(
        own_lags_kernel,
        in_specs=[in_smem] + [in_vmem] * 4,
        out_specs=in_vmem,
        out_shape=pltpu.VMEM((groups, length), jnp.float32),
        scratch_shapes=[flip_scratch],
        cost_estimate=cost(groups * OWN_WEIGHT, CORES * rows, CORES * positions, 4),
        compiler_params=params,
    )(place, *both)

    for k in rounds:
        lags = pl.pallas_call(
            functools.partial(round_lags_kernel, chips, k),
            in_specs=[in_smem] + [in_vmem] * 7,
            out_specs=in_vmem,
            out_shape=pltpu.VMEM((groups, length), jnp.float32),
            scratch_shapes=[flip_scratch],
            cost_estimate=cost(groups // 2, CORES * rows, 3 * positions, 6),
            compiler_params=params,
        )(place, *both, *[vmem(ref) for ref in first[k]], vmem(lags))

    if C1:
        for k in rounds:
            lags, second[0][k][0] = lax.optimization_barrier((lags, second[0][k][0]))

    def chip_lags(which):
        return lax.dynamic_slice_in_dim(lags, which * CORES * positions, CORES * positions, 1)

    sums = chip_lags(chip)
    for k in rounds:
        sums = sums + from_chip(chip_lags((chip - k) % chips), k, True)
    def input_part(which, offset, count, received):
        come = [ref for k in rounds for ref in first[k]]
        arrays = [ref for k in rounds for ref in received[k]]
        values = [filters, filters_peer, *come, grad_here, grad_peer, *arrays]
        return pl.pallas_call(
            functools.partial(input_grad_kernel, chips, which, offset, slot_rows),
            in_specs=[in_smem] + [in_vmem] * len(values),
            out_specs=[in_vmem] * 2,
            out_shape=[jax.ShapeDtypeStruct((sequences, count * GROUP_SIZE, positions), jnp.bfloat16)] * 2,
            scratch_shapes=[pltpu.VMEM((groups, length), jnp.float32)],
            cost_estimate=cost(count, CORES * rows, length, 4 + len(arrays)),
            compiler_params=params,
        )(place, *[vmem(value) for value in values])

    results = [
        input_part(0, 0, part_groups, first),
        input_part(1, 0, sizes[0], second[0]),
        input_part(1, sizes[0], sizes[1], second[1]),
    ]
    mine = jnp.concatenate([result[0] for result in results], axis=1)
    got = jnp.concatenate([swap_cores(result[1]) for result in results], axis=1)
    input_grad = jnp.where(
        core == 0, jnp.concatenate([mine, got], axis=1), jnp.concatenate([got, mine], axis=1)
    )

    if C2:
        sums, _ = lax.optimization_barrier((sums, results[0][0]))
    keep = lax.dynamic_slice_in_dim(sums, core * positions, positions, 1)
    got = swap_cores(lax.dynamic_slice_in_dim(sums, (1 - core) * positions, positions, 1))
    own = jnp.where(core == 0, jnp.concatenate([keep, got], axis=0), jnp.concatenate([got, keep], axis=0))
    copies = lax.axis_size("dp")
    terms = [own]
    for k in range(1, copies):
        terms.append(lax.ppermute(own, "dp", [(i, i ^ k) for i in range(copies)]))
    while len(terms) > 1:
        terms = [a + b for a, b in zip(terms[::2], terms[1::2])]
    filter_grad = terms[0]
    return (input_grad, filter_grad)


def solution(mesh):
    in_specs = (P("dp", "chan", "seq"), P("dp", "chan", "seq"), P("chan", "seq"))
    out_specs = (P("dp", "chan", "seq"), P("chan", "seq"))
    return jax.shard_map(
        per_device, mesh=mesh, in_specs=in_specs, out_specs=out_specs, check_vma=False
    )
```

```python
import functools

import jax
import jax.numpy as jnp
from jax import lax
from jax.experimental import pallas as pl
from jax.experimental.pallas import tpu as pltpu
from jax.sharding import PartitionSpec as P

GROUP_SIZE = 16
CORES = 2
VMEM_BYTES = 16 << 20
UNROLL = 16
EARLY = 14
PART_WEIGHT = 32
OWN_WEIGHT = 1000


def pick(condition, first, second):
    return jnp.where(condition, first, second)


def group_rows(ref, index, first_row=0):
    sequences, _, positions = ref.shape
    start = pl.multiple_of(first_row + index * GROUP_SIZE, GROUP_SIZE)
    return ref[:, pl.ds(start, GROUP_SIZE), :].reshape(sequences * GROUP_SIZE, positions)


def chunked(groups, body, most=UNROLL):
    count = max(size for size in range(1, most + 1) if groups % size == 0)

    def chunk(number, carry):
        body(number * count, count)
        return carry

    lax.fori_loop(0, groups // count, chunk, 0)


def input_grad_kernel(chips, which, offset, slot_rows, place, *refs):
    filter_refs, refs = refs[: CORES * chips], refs[CORES * chips :]
    own_grad, peer_grad, refs = refs[0], refs[1], refs[2:]
    round_refs, (mine, theirs, taps) = list(refs[:-3]), refs[-3:]
    core, chip = place[0], place[1]
    first_core = core == 0
    sequences, size, positions = mine.shape
    part = own_grad.shape[1] // CORES // 2
    if len(round_refs) < CORES * (chips - 1):
        round_refs = [
            ref.at[pl.ds(core_of * sequences, sequences)] for ref in round_refs for core_of in range(CORES)
        ]
    groups = size // GROUP_SIZE
    first_taps = which * (part // GROUP_SIZE) + offset
    rows = sequences * GROUP_SIZE
    width = CORES * chips * positions
    own_row = pl.multiple_of((core * 2 + which) * part + offset * GROUP_SIZE, GROUP_SIZE)
    all_groups = taps.shape[0]
    own_taps = pl.ds(pl.multiple_of(core * all_groups, all_groups), all_groups)
    holders = range(all_groups // slot_rows)
    for rotation in range(chips):
        start = lax.rem(chip + rotation, chips) * (CORES * positions)
        pair = filter_refs[CORES * rotation : CORES * (rotation + 1)]
        if rotation == 0:
            pair = [ref[own_taps, :] for ref in pair]
        else:
            pair = [
                jnp.concatenate([ref[holder, part : part + slot_rows, :] for holder in holders], axis=0)
                for ref in pair
            ]
        pair = jnp.concatenate([pick(first_core, *pair), pick(first_core, *pair[::-1])], axis=1)
        taps[:, pl.ds(pl.multiple_of(start, positions), CORES * positions)] = pair.astype(jnp.float32)
    row = lax.broadcasted_iota(jnp.int32, (positions, width), 0)
    column = lax.broadcasted_iota(jnp.int32, (positions, width), 1)
    causal = column >= row
    zeros = jnp.zeros((rows, positions), jnp.bfloat16)

    def one_group(index):
        strip = jnp.broadcast_to(taps[pl.ds(first_taps + index, 1), :], (positions, width))
        strip = pltpu.roll(strip, 0, 1, stride=1, stride_axis=0)
        strip = jnp.where(causal, strip, 0.0).astype(jnp.bfloat16)
        own, peer = group_rows(own_grad, index, own_row), group_rows(peer_grad, index, own_row)
        blocks = [pick(first_core, own, peer), pick(first_core, peer, own)]
        for distance in range(1, chips):
            received = [group_rows(ref, index) for ref in round_refs[2 * distance - 2 : 2 * distance]]
            lower = chip + distance < chips
            blocks.append(pick(lower, pick(first_core, *received), zeros))
            blocks.append(pick(lower, pick(first_core, *received[::-1]), zeros))
        grads = jnp.concatenate(
            [jnp.concatenate(blocks, axis=1), jnp.concatenate(blocks[1:] + [zeros], axis=1)], axis=0
        )
        sums = lax.dot_general(
            grads, strip, (((1,), (1,)), ((), ())), preferred_element_type=jnp.float32
        ).astype(jnp.bfloat16)
        start = pl.multiple_of(index * GROUP_SIZE, GROUP_SIZE)
        shape = (sequences, GROUP_SIZE, positions)
        early, late = sums[:rows], sums[rows:]
        mine[:, pl.ds(start, GROUP_SIZE), :] = pick(first_core, early, late).reshape(shape)
        theirs[:, pl.ds(start, GROUP_SIZE), :] = pick(first_core, late, early).reshape(shape)

    def body(first, count):
        for index in range(count):
            one_group(first + index)

    chunked(groups, body)


def reversal(positions):
    row = lax.broadcasted_iota(jnp.int32, (positions, positions), 0)
    column = lax.broadcasted_iota(jnp.int32, (positions, positions), 1)
    return (row + column == positions - 1).astype(jnp.float32).astype(jnp.bfloat16)


def flip_rows(out, core, values, flip):
    sequences, channels, positions = values.shape
    flat = values.reshape(sequences * channels, positions)
    flat = jnp.dot(flat, flip, preferred_element_type=jnp.float32).astype(jnp.bfloat16)
    out[core, :, :channels, :] = flat.reshape(sequences, channels, positions)


def lag_sums(flipped, grads, keep, lead):
    products = lax.dot_general(
        flipped, grads, (((0,), (0,)), ((), ())), preferred_element_type=jnp.float32
    )
    positions = products.shape[0]
    if keep is not None:
        products = jnp.where(keep, products, 0.0)
    if lead:
        products = jnp.concatenate([jnp.zeros((positions, lead), jnp.float32), products], axis=1)
    products = pltpu.roll(products, products.shape[1] - positions + 1, 1, stride=1, stride_axis=0)
    return jnp.sum(products, axis=0, keepdims=True)


def own_lags_kernel(place, own_input, peer_input, own_grad, peer_grad, out, flipped):
    first_core = place[0] == 0
    sequences, channels, positions = own_input.shape
    half = channels // CORES
    own_row = pl.multiple_of(place[0] * half, half)
    rows, width = sequences * GROUP_SIZE, CORES * positions
    flip = reversal(positions)
    row = lax.broadcasted_iota(jnp.int32, (positions, width), 0)
    column = lax.broadcasted_iota(jnp.int32, (positions, width), 1)
    keep = column + row >= positions - 1
    zeros = jnp.zeros((rows, positions), jnp.bfloat16)
    out[...] = jnp.zeros_like(out)

    def body(first, count):
        start = pl.multiple_of(own_row + first * GROUP_SIZE, GROUP_SIZE)
        own = own_input[:, pl.ds(start, count * GROUP_SIZE), :]
        peer = peer_input[:, pl.ds(start, count * GROUP_SIZE), :]
        flip_rows(flipped, 0, pick(first_core, own, peer), flip)
        flip_rows(flipped, 1, pick(first_core, peer, own), flip)
        for index in range(count):
            values = jnp.concatenate(
                [group_rows(flipped.at[core], index) for core in range(CORES)], axis=0
            )
            own = group_rows(own_grad, index, start)
            peer = group_rows(peer_grad, index, start)
            early, late = pick(first_core, own, peer), pick(first_core, peer, own)
            grads = jnp.concatenate(
                [jnp.concatenate([early, late], axis=1), jnp.concatenate([late, zeros], axis=1)], axis=0
            )
            out[pl.ds(first + index, 1), :width] = lag_sums(values, grads, keep, 0)

    chunked(half // GROUP_SIZE, body)


def round_lags_kernel(
    chips, distance, place, own_input, peer_input, own_grad, peer_grad, own_got, peer_got, running, out, flipped
):
    first_core = place[0] == 0
    lower = place[1] + distance < chips
    sequences, channels, positions = own_input.shape
    part = channels // CORES // 2
    rows = sequences * GROUP_SIZE
    flip = reversal(positions)
    part_row = pl.multiple_of((place[0] * 2 + jnp.where(lower, 0, 1)) * part, part)
    part_group = pl.multiple_of(jnp.where(lower, 0, part // GROUP_SIZE), part // GROUP_SIZE)
    if 2 * distance == chips:
        first_lag = (2 * distance - 2) * positions
    else:
        first_lag = pl.multiple_of(
            jnp.where(lower, 2 * distance - 2, 2 * (chips - distance) - 2) * positions, positions
        )
    zeros = jnp.zeros((rows, positions), jnp.bfloat16)
    out[...] = running[...]

    def body(first, count):
        start = pl.multiple_of(first * GROUP_SIZE, GROUP_SIZE)
        own_rows = pl.ds(pl.multiple_of(part_row + start, GROUP_SIZE), count * GROUP_SIZE)
        got_rows = pl.ds(start, count * GROUP_SIZE)
        own = pick(lower, own_input[:, own_rows, :], own_got[:, got_rows, :])
        peer = pick(lower, peer_input[:, own_rows, :], peer_got[:, got_rows, :])
        flip_rows(flipped, 0, pick(first_core, own, peer), flip)
        flip_rows(flipped, 1, pick(first_core, peer, own), flip)
        for index in range(count):
            got = group_rows(own_got, index, start), group_rows(peer_got, index, start)
            grads = (
                group_rows(own_grad, index, part_row + start),
                group_rows(peer_grad, index, part_row + start),
            )
            right = [pick(lower, b, a) for a, b in zip(grads, got)]
            values = jnp.concatenate(
                [group_rows(flipped.at[core], index) for core in range(CORES)], axis=0
            )
            early, late = pick(first_core, *right), pick(first_core, *right[::-1])
            pairs = jnp.concatenate(
                [
                    jnp.concatenate([zeros, early, late], axis=1),
                    jnp.concatenate([early, late, zeros], axis=1),
                ],
                axis=0,
            )
            where = (pl.ds(part_group + first + index, 1), pl.ds(first_lag, 2 * CORES * positions))
            out[where] = out[where] + lag_sums(values, pairs, None, positions)

    chunked(part // GROUP_SIZE, body, 2 * UNROLL)


def assemble_kernel(out_place, *refs):
    parts, out, sems = refs[:-2], refs[-2], refs[-1]
    half = out.shape[1] // CORES
    core = out_place[0]
    copies = []
    start = core * half
    for number, ref in enumerate(parts):
        if number == len(parts) // 2:
            start = (1 - core) * half
        rows = pl.ds(pl.multiple_of(start, GROUP_SIZE), ref.shape[1])
        copies.append(pltpu.make_async_copy(ref, out.at[:, rows, :], sems.at[number]))
        start = start + ref.shape[1]
    for copy in copies:
        copy.start()
    for copy in copies:
        copy.wait()


def parts_kernel(chips, slot_rows, inputs, output_grad, filters, *refs):
    count = CORES * (chips - 1)
    outs, stages, in_sems, out_sems = refs[:count], refs[count : 2 * count], refs[-2], refs[-1]
    sequences = inputs.shape[0]
    half = inputs.shape[1] // CORES
    part = half // 2
    groups = filters.shape[0] // CORES
    own_index = lax.axis_index("seq")
    chip, core = lax.div(own_index, CORES), lax.rem(own_index, CORES)

    def arrival(source, start, target, number):
        return pltpu.make_async_copy(
            source.at[:, pl.ds(pl.multiple_of(start, GROUP_SIZE), part), :],
            target.at[:, pl.ds(0, part), :],
            in_sems.at[number],
        )

    for number in range(count):
        distance, other = number // CORES + 1, number % CORES
        whose = core if other == 0 else 1 - core
        start = whose * half
        target = stages[number]
        for sequence in range(sequences):
            slot = sequence if slot_rows < groups else 0
            row = pl.multiple_of(whose * groups + slot * slot_rows, GROUP_SIZE)
            pltpu.make_async_copy(
                filters.at[pl.ds(row, slot_rows), :],
                target.at[sequence, pl.ds(part, slot_rows), :],
                in_sems.at[number],
            ).start()
        lax.cond(
            chip >= distance,
            lambda: arrival(output_grad, start, target, number).start(),
            lambda: arrival(inputs, start + part, target, number).start(),
        )
    for number in range(count):
        pltpu.make_async_copy(stages[number], stages[number], in_sems.at[number]).wait()
        pltpu.make_async_copy(stages[number], outs[number], out_sems.at[number]).start()
    for number in range(count):
        pltpu.make_async_copy(stages[number], outs[number], out_sems.at[number]).wait()


def second_kernel(own_grad, peer_grad, *refs):
    outs, sems = refs[:-1], refs[-1]
    sequences = own_grad.shape[0]
    half = own_grad.shape[1] // CORES
    core = lax.rem(lax.axis_index("seq"), CORES)
    start = core * half + half // 2
    copies = []
    for out in outs:
        for number, ref in enumerate((own_grad, peer_grad)):
            copies.append(
                pltpu.make_async_copy(
                    ref.at[:, pl.ds(pl.multiple_of(start, GROUP_SIZE), out.shape[1]), :],
                    out.at[pl.ds(number * sequences, sequences)],
                    sems.at[len(copies)],
                )
            )
        start = start + out.shape[1]
    for copy in copies:
        copy.start()
    for copy in copies:
        copy.wait()


def per_device(inputs, output_grad, filters):
    sequences, channels, positions = inputs.shape
    shard_count = lax.axis_size("seq")
    chips = shard_count // CORES
    own_index = lax.axis_index("seq")
    chip, core = own_index // CORES, own_index % CORES
    place = jnp.stack([core, chip]).astype(jnp.int32)
    half = channels // CORES
    part = half // 2
    groups = half // GROUP_SIZE
    slot_rows = groups // 2 if sequences == 2 and groups % (2 * GROUP_SIZE) == 0 else groups
    length = shard_count * positions
    rows = sequences * GROUP_SIZE
    rounds = range(1, chips)

    def swap_cores(value):
        return lax.ppermute(value, "seq", [(i, i ^ 1) for i in range(shard_count)])

    def from_chip(value, distance, wrap, other=0):
        pairs = [
            (i, (i - distance * CORES) % shard_count ^ other)
            for i in range(shard_count)
            if wrap or i >= distance * CORES
        ]
        return lax.ppermute(value, "seq", pairs)

    in_hbm = pl.BlockSpec(memory_space=pltpu.HBM)
    params = pltpu.CompilerParams(vmem_limit_bytes=VMEM_BYTES)

    heights = [part + slot_rows] * (CORES * (chips - 1))
    outgoing = pl.pallas_call(
        functools.partial(parts_kernel, chips, slot_rows),
        in_specs=[in_hbm] * 3,
        out_specs=[in_hbm] * len(heights),
        out_shape=[jax.ShapeDtypeStruct((sequences, height, positions), inputs.dtype) for height in heights],
        scratch_shapes=[pltpu.VMEM((sequences, height, positions), inputs.dtype) for height in heights]
        + [pltpu.SemaphoreType.DMA((len(heights),))] * 2,
    )(inputs, output_grad, filters)

    to_swap = (filters, output_grad, inputs)
    filters_peer, grad_peer, input_peer = (swap_cores(value) for value in to_swap)
    first = {
        k: [from_chip(outgoing[CORES * (k - 1) + other], k, True, other) for other in range(CORES)]
        for k in rounds
    }

    in_smem, in_vmem = pl.BlockSpec(memory_space=pltpu.SMEM), pl.BlockSpec(memory_space=pltpu.VMEM)
    flip_scratch = pltpu.VMEM((CORES, sequences, 2 * UNROLL * GROUP_SIZE, positions), jnp.bfloat16)

    def vmem(value):
        return pltpu.with_memory_space_constraint(value, pltpu.VMEM)

    def cost(group_count, depth, width, arrays):
        return pl.CostEstimate(
            flops=max(1, int(2 * group_count * depth * positions * width)),
            bytes_accessed=max(1, int(arrays * group_count * rows * positions * 2)),
            transcendentals=0,
        )

    input_here, grad_here = vmem(inputs), vmem(output_grad)
    input_peer, grad_peer = vmem(input_peer), vmem(grad_peer)
    both = (input_here, input_peer, grad_here, grad_peer)
    part_groups = groups // 2
    early_groups = part_groups * EARLY // 32
    sizes = [early_groups, part_groups - early_groups]
    outgoing = pl.pallas_call(
        second_kernel,
        in_specs=[in_vmem] * 2,
        out_specs=[in_hbm] * len(sizes),
        out_shape=[
            jax.ShapeDtypeStruct((CORES * sequences, size * GROUP_SIZE, positions), inputs.dtype) for size in sizes
        ],
        scratch_shapes=[pltpu.SemaphoreType.DMA((CORES * len(sizes),))],
    )(grad_here, grad_peer)
    second = [{k: [from_chip(outgoing[0], k, False)] for k in rounds}]

    lags = pl.pallas_call(
        own_lags_kernel,
        in_specs=[in_smem] + [in_vmem] * 4,
        out_specs=in_vmem,
        out_shape=pltpu.VMEM((groups, length), jnp.float32),
        scratch_shapes=[flip_scratch],
        cost_estimate=cost(groups * OWN_WEIGHT, CORES * rows, CORES * positions, 4),
        compiler_params=params,
    )(place, *both)

    for k in rounds:
        lags = pl.pallas_call(
            functools.partial(round_lags_kernel, chips, k),
            in_specs=[in_smem] + [in_vmem] * 7,
            out_specs=in_vmem,
            out_shape=pltpu.VMEM((groups, length), jnp.float32),
            scratch_shapes=[flip_scratch],
            cost_estimate=cost(groups // 2, CORES * rows, 3 * positions, 6),
            compiler_params=params,
        )(place, *both, *[vmem(ref) for ref in first[k]], vmem(lags))

    for k in rounds:
        lags, second[0][k][0] = lax.optimization_barrier((lags, second[0][k][0]))

    def chip_lags(which):
        return lax.dynamic_slice_in_dim(lags, which * CORES * positions, CORES * positions, 1)

    sums = chip_lags(chip)
    for k in rounds:
        sums = sums + from_chip(chip_lags((chip - k) % chips), k, True)

    def input_part(which, offset, count, received):
        come = [ref for k in rounds for ref in first[k]]
        arrays = [ref for k in rounds for ref in received[k]]
        values = [filters, filters_peer, *come, grad_here, grad_peer, *arrays]
        return pl.pallas_call(
            functools.partial(input_grad_kernel, chips, which, offset, slot_rows),
            in_specs=[in_smem] + [in_vmem] * len(values),
            out_specs=[in_vmem] * 2,
            out_shape=[jax.ShapeDtypeStruct((sequences, count * GROUP_SIZE, positions), jnp.bfloat16)] * 2,
            scratch_shapes=[pltpu.VMEM((groups, length), jnp.float32)],
            cost_estimate=cost(count if which and offset else PART_WEIGHT, CORES * rows, length, 4 + len(arrays)),
            compiler_params=params,
        )(place, *[vmem(value) for value in values])

    second.append({k: [from_chip(outgoing[1], k, False)] for k in rounds})
    for k in rounds:
        second[1][k][0], second[0][k][0] = lax.optimization_barrier((second[1][k][0], second[0][k][0]))
    results = [
        input_part(0, 0, part_groups, first),
        input_part(1, 0, sizes[0], second[0]),
        input_part(1, sizes[0], sizes[1], second[1]),
    ]
    sums, _ = lax.optimization_barrier((sums, results[0][0]))
    mine = jnp.concatenate([result[0] for result in results], axis=1)
    got = jnp.concatenate([swap_cores(result[1]) for result in results], axis=1)
    input_grad = jnp.where(
        core == 0, jnp.concatenate([mine, got], axis=1), jnp.concatenate([got, mine], axis=1)
    )

    keep = lax.dynamic_slice_in_dim(sums, core * positions, positions, 1)
    got = swap_cores(lax.dynamic_slice_in_dim(sums, (1 - core) * positions, positions, 1))
    own = jnp.where(core == 0, jnp.concatenate([keep, got], axis=0), jnp.concatenate([got, keep], axis=0))
    copies = lax.axis_size("dp")
    terms = [own]
    for k in range(1, copies):
        terms.append(lax.ppermute(own, "dp", [(i, i ^ k) for i in range(copies)]))
    while len(terms) > 1:
        terms = [a + b for a, b in zip(terms[::2], terms[1::2])]
    filter_grad = terms[0]
    return (input_grad, filter_grad)


def solution(mesh):
    in_specs = (P("dp", "chan", "seq"), P("dp", "chan", "seq"), P("chan", "seq"))
    out_specs = (P("dp", "chan", "seq"), P("chan", "seq"))
    return jax.shard_map(
        per_device, mesh=mesh, in_specs=in_specs, out_specs=out_specs, check_vma=False
    )
```

```python
import functools

import jax
import jax.numpy as jnp
from jax import lax
from jax.experimental import pallas as pl
from jax.experimental.pallas import tpu as pltpu
from jax.sharding import PartitionSpec as P

GROUP_SIZE = 16
CORES = 2
VMEM_BYTES = 16 << 20
UNROLL = 16
EARLY = 14
PART_WEIGHT = 32
OWN_WEIGHT = 1000


def pick(condition, first, second):
    return jnp.where(condition, first, second)


def group_rows(ref, index, first_row=0):
    sequences, _, positions = ref.shape
    start = pl.multiple_of(first_row + index * GROUP_SIZE, GROUP_SIZE)
    return ref[:, pl.ds(start, GROUP_SIZE), :].reshape(sequences * GROUP_SIZE, positions)


def chunked(groups, body, most=UNROLL):
    count = max(size for size in range(1, most + 1) if groups % size == 0)

    def chunk(number, carry):
        body(number * count, count)
        return carry

    lax.fori_loop(0, groups // count, chunk, 0)


def input_grad_kernel(chips, which, offset, slot_rows, place, *refs):
    filter_refs, refs = refs[: CORES * chips], refs[CORES * chips :]
    own_grad, peer_grad, refs = refs[0], refs[1], refs[2:]
    round_refs, (mine, theirs, taps) = list(refs[:-3]), refs[-3:]
    core, chip = place[0], place[1]
    first_core = core == 0
    sequences, size, positions = mine.shape
    part = own_grad.shape[1] // CORES // 2
    if len(round_refs) < CORES * (chips - 1):
        round_refs = [
            ref.at[pl.ds(core_of * sequences, sequences)] for ref in round_refs for core_of in range(CORES)
        ]
    groups = size // GROUP_SIZE
    first_taps = which * (part // GROUP_SIZE) + offset
    rows = sequences * GROUP_SIZE
    width = CORES * chips * positions
    own_row = pl.multiple_of((core * 2 + which) * part + offset * GROUP_SIZE, GROUP_SIZE)
    all_groups = taps.shape[0]
    own_taps = pl.ds(pl.multiple_of(core * all_groups, all_groups), all_groups)
    holders = range(all_groups // slot_rows)
    for rotation in range(chips):
        start = lax.rem(chip + rotation, chips) * (CORES * positions)
        pair = filter_refs[CORES * rotation : CORES * (rotation + 1)]
        if rotation == 0:
            pair = [ref[own_taps, :] for ref in pair]
        else:
            pair = [
                jnp.concatenate([ref[holder, part : part + slot_rows, :] for holder in holders], axis=0)
                for ref in pair
            ]
        pair = jnp.concatenate([pick(first_core, *pair), pick(first_core, *pair[::-1])], axis=1)
        taps[:, pl.ds(pl.multiple_of(start, positions), CORES * positions)] = pair.astype(jnp.float32)
    row = lax.broadcasted_iota(jnp.int32, (positions, width), 0)
    column = lax.broadcasted_iota(jnp.int32, (positions, width), 1)
    causal = column >= row
    zeros = jnp.zeros((rows, positions), jnp.bfloat16)

    def one_group(index):
        strip = jnp.broadcast_to(taps[pl.ds(first_taps + index, 1), :], (positions, width))
        strip = pltpu.roll(strip, 0, 1, stride=1, stride_axis=0)
        strip = jnp.where(causal, strip, 0.0).astype(jnp.bfloat16)
        own, peer = group_rows(own_grad, index, own_row), group_rows(peer_grad, index, own_row)
        blocks = [pick(first_core, own, peer), pick(first_core, peer, own)]
        for distance in range(1, chips):
            received = [group_rows(ref, index) for ref in round_refs[2 * distance - 2 : 2 * distance]]
            lower = chip + distance < chips
            blocks.append(pick(lower, pick(first_core, *received), zeros))
            blocks.append(pick(lower, pick(first_core, *received[::-1]), zeros))
        grads = jnp.concatenate(
            [jnp.concatenate(blocks, axis=1), jnp.concatenate(blocks[1:] + [zeros], axis=1)], axis=0
        )
        sums = lax.dot_general(
            grads, strip, (((1,), (1,)), ((), ())), preferred_element_type=jnp.float32
        ).astype(jnp.bfloat16)
        start = pl.multiple_of(index * GROUP_SIZE, GROUP_SIZE)
        shape = (sequences, GROUP_SIZE, positions)
        early, late = sums[:rows], sums[rows:]
        mine[:, pl.ds(start, GROUP_SIZE), :] = pick(first_core, early, late).reshape(shape)
        theirs[:, pl.ds(start, GROUP_SIZE), :] = pick(first_core, late, early).reshape(shape)

    def body(first, count):
        for index in range(count):
            one_group(first + index)

    chunked(groups, body, 2 * UNROLL)


def reversal(positions):
    row = lax.broadcasted_iota(jnp.int32, (positions, positions), 0)
    column = lax.broadcasted_iota(jnp.int32, (positions, positions), 1)
    return (row + column == positions - 1).astype(jnp.float32).astype(jnp.bfloat16)


def flip_rows(out, core, values, flip):
    sequences, channels, positions = values.shape
    flat = values.reshape(sequences * channels, positions)
    flat = jnp.dot(flat, flip, preferred_element_type=jnp.float32).astype(jnp.bfloat16)
    out[core, :, :channels, :] = flat.reshape(sequences, channels, positions)


def lag_sums(flipped, grads, keep, lead):
    products = lax.dot_general(
        flipped, grads, (((0,), (0,)), ((), ())), preferred_element_type=jnp.float32
    )
    positions = products.shape[0]
    if keep is not None:
        products = jnp.where(keep, products, 0.0)
    if lead:
        products = jnp.concatenate([jnp.zeros((positions, lead), jnp.float32), products], axis=1)
    products = pltpu.roll(products, products.shape[1] - positions + 1, 1, stride=1, stride_axis=0)
    return jnp.sum(products, axis=0, keepdims=True)


def own_lags_kernel(place, own_input, peer_input, own_grad, peer_grad, out, flipped):
    first_core = place[0] == 0
    sequences, channels, positions = own_input.shape
    half = channels // CORES
    own_row = pl.multiple_of(place[0] * half, half)
    rows, width = sequences * GROUP_SIZE, CORES * positions
    flip = reversal(positions)
    row = lax.broadcasted_iota(jnp.int32, (positions, width), 0)
    column = lax.broadcasted_iota(jnp.int32, (positions, width), 1)
    keep = column + row >= positions - 1
    zeros = jnp.zeros((rows, positions), jnp.bfloat16)
    out[...] = jnp.zeros_like(out)

    def body(first, count):
        start = pl.multiple_of(own_row + first * GROUP_SIZE, GROUP_SIZE)
        own = own_input[:, pl.ds(start, count * GROUP_SIZE), :]
        peer = peer_input[:, pl.ds(start, count * GROUP_SIZE), :]
        flip_rows(flipped, 0, pick(first_core, own, peer), flip)
        flip_rows(flipped, 1, pick(first_core, peer, own), flip)
        for index in range(count):
            values = jnp.concatenate(
                [group_rows(flipped.at[core], index) for core in range(CORES)], axis=0
            )
            own = group_rows(own_grad, index, start)
            peer = group_rows(peer_grad, index, start)
            early, late = pick(first_core, own, peer), pick(first_core, peer, own)
            grads = jnp.concatenate(
                [jnp.concatenate([early, late], axis=1), jnp.concatenate([late, zeros], axis=1)], axis=0
            )
            out[pl.ds(first + index, 1), :width] = lag_sums(values, grads, keep, 0)

    chunked(half // GROUP_SIZE, body)


def round_lags_kernel(
    chips, distance, place, own_input, peer_input, own_grad, peer_grad, own_got, peer_got, running, out, flipped
):
    first_core = place[0] == 0
    lower = place[1] + distance < chips
    sequences, channels, positions = own_input.shape
    part = channels // CORES // 2
    rows = sequences * GROUP_SIZE
    flip = reversal(positions)
    part_row = pl.multiple_of((place[0] * 2 + jnp.where(lower, 0, 1)) * part, part)
    part_group = pl.multiple_of(jnp.where(lower, 0, part // GROUP_SIZE), part // GROUP_SIZE)
    if 2 * distance == chips:
        first_lag = (2 * distance - 2) * positions
    else:
        first_lag = pl.multiple_of(
            jnp.where(lower, 2 * distance - 2, 2 * (chips - distance) - 2) * positions, positions
        )
    zeros = jnp.zeros((rows, positions), jnp.bfloat16)
    out[...] = running[...]

    def body(first, count):
        start = pl.multiple_of(first * GROUP_SIZE, GROUP_SIZE)
        own_rows = pl.ds(pl.multiple_of(part_row + start, GROUP_SIZE), count * GROUP_SIZE)
        got_rows = pl.ds(start, count * GROUP_SIZE)
        own = pick(lower, own_input[:, own_rows, :], own_got[:, got_rows, :])
        peer = pick(lower, peer_input[:, own_rows, :], peer_got[:, got_rows, :])
        flip_rows(flipped, 0, pick(first_core, own, peer), flip)
        flip_rows(flipped, 1, pick(first_core, peer, own), flip)
        for index in range(count):
            got = group_rows(own_got, index, start), group_rows(peer_got, index, start)
            grads = (
                group_rows(own_grad, index, part_row + start),
                group_rows(peer_grad, index, part_row + start),
            )
            right = [pick(lower, b, a) for a, b in zip(grads, got)]
            values = jnp.concatenate(
                [group_rows(flipped.at[core], index) for core in range(CORES)], axis=0
            )
            early, late = pick(first_core, *right), pick(first_core, *right[::-1])
            pairs = jnp.concatenate(
                [
                    jnp.concatenate([zeros, early, late], axis=1),
                    jnp.concatenate([early, late, zeros], axis=1),
                ],
                axis=0,
            )
            where = (pl.ds(part_group + first + index, 1), pl.ds(first_lag, 2 * CORES * positions))
            out[where] = out[where] + lag_sums(values, pairs, None, positions)

    chunked(part // GROUP_SIZE, body, 2 * UNROLL)


def assemble_kernel(out_place, *refs):
    parts, out, sems = refs[:-2], refs[-2], refs[-1]
    half = out.shape[1] // CORES
    core = out_place[0]
    copies = []
    start = core * half
    for number, ref in enumerate(parts):
        if number == len(parts) // 2:
            start = (1 - core) * half
        rows = pl.ds(pl.multiple_of(start, GROUP_SIZE), ref.shape[1])
        copies.append(pltpu.make_async_copy(ref, out.at[:, rows, :], sems.at[number]))
        start = start + ref.shape[1]
    for copy in copies:
        copy.start()
    for copy in copies:
        copy.wait()


def parts_kernel(chips, slot_rows, inputs, output_grad, filters, *refs):
    count = CORES * (chips - 1)
    outs, stages, in_sems, out_sems = refs[:count], refs[count : 2 * count], refs[-2], refs[-1]
    sequences = inputs.shape[0]
    half = inputs.shape[1] // CORES
    part = half // 2
    groups = filters.shape[0] // CORES
    own_index = lax.axis_index("seq")
    chip, core = lax.div(own_index, CORES), lax.rem(own_index, CORES)

    def arrival(source, start, target, number):
        return pltpu.make_async_copy(
            source.at[:, pl.ds(pl.multiple_of(start, GROUP_SIZE), part), :],
            target.at[:, pl.ds(0, part), :],
            in_sems.at[number],
        )

    for number in range(count):
        distance, other = number // CORES + 1, number % CORES
        whose = core if other == 0 else 1 - core
        start = whose * half
        target = stages[number]
        for sequence in range(sequences):
            slot = sequence if slot_rows < groups else 0
            row = pl.multiple_of(whose * groups + slot * slot_rows, GROUP_SIZE)
            pltpu.make_async_copy(
                filters.at[pl.ds(row, slot_rows), :],
                target.at[sequence, pl.ds(part, slot_rows), :],
                in_sems.at[number],
            ).start()
        lax.cond(
            chip >= distance,
            lambda: arrival(output_grad, start, target, number).start(),
            lambda: arrival(inputs, start + part, target, number).start(),
        )
    for number in range(count):
        pltpu.make_async_copy(stages[number], stages[number], in_sems.at[number]).wait()
        pltpu.make_async_copy(stages[number], outs[number], out_sems.at[number]).start()
    for number in range(count):
        pltpu.make_async_copy(stages[number], outs[number], out_sems.at[number]).wait()


def second_kernel(own_grad, peer_grad, *refs):
    outs, sems = refs[:-1], refs[-1]
    sequences = own_grad.shape[0]
    half = own_grad.shape[1] // CORES
    core = lax.rem(lax.axis_index("seq"), CORES)
    start = core * half + half // 2
    copies = []
    for out in outs:
        for number, ref in enumerate((own_grad, peer_grad)):
            copies.append(
                pltpu.make_async_copy(
                    ref.at[:, pl.ds(pl.multiple_of(start, GROUP_SIZE), out.shape[1]), :],
                    out.at[pl.ds(number * sequences, sequences)],
                    sems.at[len(copies)],
                )
            )
        start = start + out.shape[1]
    for copy in copies:
        copy.start()
    for copy in copies:
        copy.wait()


def per_device(inputs, output_grad, filters):
    sequences, channels, positions = inputs.shape
    shard_count = lax.axis_size("seq")
    chips = shard_count // CORES
    own_index = lax.axis_index("seq")
    chip, core = own_index // CORES, own_index % CORES
    place = jnp.stack([core, chip]).astype(jnp.int32)
    half = channels // CORES
    part = half // 2
    groups = half // GROUP_SIZE
    slot_rows = groups // 2 if sequences == 2 and groups % (2 * GROUP_SIZE) == 0 else groups
    length = shard_count * positions
    rows = sequences * GROUP_SIZE
    rounds = range(1, chips)

    def swap_cores(value):
        return lax.ppermute(value, "seq", [(i, i ^ 1) for i in range(shard_count)])

    def from_chip(value, distance, wrap, other=0):
        pairs = [
            (i, (i - distance * CORES) % shard_count ^ other)
            for i in range(shard_count)
            if wrap or i >= distance * CORES
        ]
        return lax.ppermute(value, "seq", pairs)

    in_hbm = pl.BlockSpec(memory_space=pltpu.HBM)
    params = pltpu.CompilerParams(vmem_limit_bytes=VMEM_BYTES)

    heights = [part + slot_rows] * (CORES * (chips - 1))
    outgoing = pl.pallas_call(
        functools.partial(parts_kernel, chips, slot_rows),
        in_specs=[in_hbm] * 3,
        out_specs=[in_hbm] * len(heights),
        out_shape=[jax.ShapeDtypeStruct((sequences, height, positions), inputs.dtype) for height in heights],
        scratch_shapes=[pltpu.VMEM((sequences, height, positions), inputs.dtype) for height in heights]
        + [pltpu.SemaphoreType.DMA((len(heights),))] * 2,
    )(inputs, output_grad, filters)

    to_swap = (filters, output_grad, inputs)
    filters_peer, grad_peer, input_peer = (swap_cores(value) for value in to_swap)
    first = {
        k: [from_chip(outgoing[CORES * (k - 1) + other], k, True, other) for other in range(CORES)]
        for k in rounds
    }

    in_smem, in_vmem = pl.BlockSpec(memory_space=pltpu.SMEM), pl.BlockSpec(memory_space=pltpu.VMEM)
    flip_scratch = pltpu.VMEM((CORES, sequences, 2 * UNROLL * GROUP_SIZE, positions), jnp.bfloat16)

    def vmem(value):
        return pltpu.with_memory_space_constraint(value, pltpu.VMEM)

    def cost(group_count, depth, width, arrays):
        return pl.CostEstimate(
            flops=max(1, int(2 * group_count * depth * positions * width)),
            bytes_accessed=max(1, int(arrays * group_count * rows * positions * 2)),
            transcendentals=0,
        )

    input_here, grad_here = vmem(inputs), vmem(output_grad)
    input_peer, grad_peer = vmem(input_peer), vmem(grad_peer)
    both = (input_here, input_peer, grad_here, grad_peer)
    part_groups = groups // 2
    early_groups = part_groups * EARLY // 32
    sizes = [early_groups, part_groups - early_groups]
    outgoing = pl.pallas_call(
        second_kernel,
        in_specs=[in_vmem] * 2,
        out_specs=[in_hbm] * len(sizes),
        out_shape=[
            jax.ShapeDtypeStruct((CORES * sequences, size * GROUP_SIZE, positions), inputs.dtype) for size in sizes
        ],
        scratch_shapes=[pltpu.SemaphoreType.DMA((CORES * len(sizes),))],
    )(grad_here, grad_peer)
    second = [{k: [from_chip(outgoing[0], k, False)] for k in rounds}]

    lags = pl.pallas_call(
        own_lags_kernel,
        in_specs=[in_smem] + [in_vmem] * 4,
        out_specs=in_vmem,
        out_shape=pltpu.VMEM((groups, length), jnp.float32),
        scratch_shapes=[flip_scratch],
        cost_estimate=cost(groups * OWN_WEIGHT, CORES * rows, CORES * positions, 4),
        compiler_params=params,
    )(place, *both)

    for k in rounds:
        lags = pl.pallas_call(
            functools.partial(round_lags_kernel, chips, k),
            in_specs=[in_smem] + [in_vmem] * 7,
            out_specs=in_vmem,
            out_shape=pltpu.VMEM((groups, length), jnp.float32),
            scratch_shapes=[flip_scratch],
            cost_estimate=cost(groups // 2, CORES * rows, 3 * positions, 6),
            compiler_params=params,
        )(place, *both, *[vmem(ref) for ref in first[k]], vmem(lags))

    for k in rounds:
        lags, second[0][k][0] = lax.optimization_barrier((lags, second[0][k][0]))

    def chip_lags(which):
        return lax.dynamic_slice_in_dim(lags, which * CORES * positions, CORES * positions, 1)

    sums = chip_lags(chip)
    for k in rounds:
        sums = sums + from_chip(chip_lags((chip - k) % chips), k, True)

    def input_part(which, offset, count, received):
        come = [ref for k in rounds for ref in first[k]]
        arrays = [ref for k in rounds for ref in received[k]]
        values = [filters, filters_peer, *come, grad_here, grad_peer, *arrays]
        return pl.pallas_call(
            functools.partial(input_grad_kernel, chips, which, offset, slot_rows),
            in_specs=[in_smem] + [in_vmem] * len(values),
            out_specs=[in_vmem] * 2,
            out_shape=[jax.ShapeDtypeStruct((sequences, count * GROUP_SIZE, positions), jnp.bfloat16)] * 2,
            scratch_shapes=[pltpu.VMEM((groups, length), jnp.float32)],
            cost_estimate=cost(count if which and offset else PART_WEIGHT, CORES * rows, length, 4 + len(arrays)),
            compiler_params=params,
        )(place, *[vmem(value) for value in values])

    second.append({k: [from_chip(outgoing[1], k, False)] for k in rounds})
    for k in rounds:
        second[1][k][0], second[0][k][0] = lax.optimization_barrier((second[1][k][0], second[0][k][0]))
    results = [
        input_part(0, 0, part_groups, first),
        input_part(1, 0, sizes[0], second[0]),
        input_part(1, sizes[0], sizes[1], second[1]),
    ]
    sums, _ = lax.optimization_barrier((sums, results[0][0]))
    mine = jnp.concatenate([result[0] for result in results], axis=1)
    got = jnp.concatenate([swap_cores(result[1]) for result in results], axis=1)
    input_grad = jnp.where(
        core == 0, jnp.concatenate([mine, got], axis=1), jnp.concatenate([got, mine], axis=1)
    )

    keep = lax.dynamic_slice_in_dim(sums, core * positions, positions, 1)
    got = swap_cores(lax.dynamic_slice_in_dim(sums, (1 - core) * positions, positions, 1))
    own = jnp.where(core == 0, jnp.concatenate([keep, got], axis=0), jnp.concatenate([got, keep], axis=0))
    copies = lax.axis_size("dp")
    terms = [own]
    for k in range(1, copies):
        terms.append(lax.ppermute(own, "dp", [(i, i ^ k) for i in range(copies)]))
    while len(terms) > 1:
        terms = [a + b for a, b in zip(terms[::2], terms[1::2])]
    filter_grad = terms[0]
    return (input_grad, filter_grad)


def solution(mesh):
    in_specs = (P("dp", "chan", "seq"), P("dp", "chan", "seq"), P("chan", "seq"))
    out_specs = (P("dp", "chan", "seq"), P("chan", "seq"))
    return jax.shard_map(
        per_device, mesh=mesh, in_specs=in_specs, out_specs=out_specs, check_vma=False
    )
```

```python
import functools

import jax
import jax.numpy as jnp
from jax import lax
from jax.experimental import pallas as pl
from jax.experimental.pallas import tpu as pltpu
from jax.sharding import PartitionSpec as P

GROUP_SIZE = 16
CORES = 2
VMEM_BYTES = 16 << 20
UNROLL = 16
EARLY = 14
PART_WEIGHT = 32
OWN_WEIGHT = 1000


def pick(condition, first, second):
    return jnp.where(condition, first, second)


def group_rows(ref, index, first_row=0):
    sequences, _, positions = ref.shape
    start = pl.multiple_of(first_row + index * GROUP_SIZE, GROUP_SIZE)
    return ref[:, pl.ds(start, GROUP_SIZE), :].reshape(sequences * GROUP_SIZE, positions)


def chunked(groups, body, most=UNROLL):
    count = max(size for size in range(1, most + 1) if groups % size == 0)

    def chunk(number, carry):
        body(number * count, count)
        return carry

    lax.fori_loop(0, groups // count, chunk, 0)


def input_grad_kernel(chips, which, offset, slot_rows, place, *refs):
    filter_refs, refs = refs[: CORES * chips], refs[CORES * chips :]
    own_grad, peer_grad, refs = refs[0], refs[1], refs[2:]
    round_refs, (mine, theirs, taps) = list(refs[:-3]), refs[-3:]
    core, chip = place[0], place[1]
    first_core = core == 0
    sequences, size, positions = mine.shape
    part = own_grad.shape[1] // CORES // 2
    if len(round_refs) < CORES * (chips - 1):
        round_refs = [
            ref.at[pl.ds(core_of * sequences, sequences)] for ref in round_refs for core_of in range(CORES)
        ]
    groups = size // GROUP_SIZE
    first_taps = which * (part // GROUP_SIZE) + offset
    rows = sequences * GROUP_SIZE
    width = CORES * chips * positions
    own_row = pl.multiple_of((core * 2 + which) * part + offset * GROUP_SIZE, GROUP_SIZE)
    all_groups = taps.shape[0]
    own_taps = pl.ds(pl.multiple_of(core * all_groups, all_groups), all_groups)
    holders = range(all_groups // slot_rows)
    for rotation in range(chips):
        start = lax.rem(chip + rotation, chips) * (CORES * positions)
        pair = filter_refs[CORES * rotation : CORES * (rotation + 1)]
        if rotation == 0:
            pair = [ref[own_taps, :] for ref in pair]
        else:
            pair = [
                jnp.concatenate([ref[holder, part : part + slot_rows, :] for holder in holders], axis=0)
                for ref in pair
            ]
        pair = jnp.concatenate([pick(first_core, *pair), pick(first_core, *pair[::-1])], axis=1)
        taps[:, pl.ds(pl.multiple_of(start, positions), CORES * positions)] = pair.astype(jnp.float32)
    row = lax.broadcasted_iota(jnp.int32, (positions, width), 0)
    column = lax.broadcasted_iota(jnp.int32, (positions, width), 1)
    causal = column >= row
    zeros = jnp.zeros((rows, positions), jnp.bfloat16)

    def one_group(index):
        strip = jnp.broadcast_to(taps[pl.ds(first_taps + index, 1), :], (positions, width))
        strip = pltpu.roll(strip, 0, 1, stride=1, stride_axis=0)
        strip = jnp.where(causal, strip, 0.0).astype(jnp.bfloat16)
        own, peer = group_rows(own_grad, index, own_row), group_rows(peer_grad, index, own_row)
        blocks = [pick(first_core, own, peer), pick(first_core, peer, own)]
        for distance in range(1, chips):
            received = [group_rows(ref, index) for ref in round_refs[2 * distance - 2 : 2 * distance]]
            lower = chip + distance < chips
            blocks.append(pick(lower, pick(first_core, *received), zeros))
            blocks.append(pick(lower, pick(first_core, *received[::-1]), zeros))
        grads = jnp.concatenate(
            [jnp.concatenate(blocks, axis=1), jnp.concatenate(blocks[1:] + [zeros], axis=1)], axis=0
        )
        sums = lax.dot_general(
            grads, strip, (((1,), (1,)), ((), ())), preferred_element_type=jnp.float32
        ).astype(jnp.bfloat16)
        start = pl.multiple_of(index * GROUP_SIZE, GROUP_SIZE)
        shape = (sequences, GROUP_SIZE, positions)
        early, late = sums[:rows], sums[rows:]
        mine[:, pl.ds(start, GROUP_SIZE), :] = pick(first_core, early, late).reshape(shape)
        theirs[:, pl.ds(start, GROUP_SIZE), :] = pick(first_core, late, early).reshape(shape)

    def body(first, count):
        for index in range(count):
            one_group(first + index)

    chunked(groups, body)


def reversal(positions):
    row = lax.broadcasted_iota(jnp.int32, (positions, positions), 0)
    column = lax.broadcasted_iota(jnp.int32, (positions, positions), 1)
    return (row + column == positions - 1).astype(jnp.float32).astype(jnp.bfloat16)


def flip_rows(out, core, values, flip):
    sequences, channels, positions = values.shape
    flat = values.reshape(sequences * channels, positions)
    flat = jnp.dot(flat, flip, preferred_element_type=jnp.float32).astype(jnp.bfloat16)
    out[core, :, :channels, :] = flat.reshape(sequences, channels, positions)


def lag_sums(flipped, grads, keep, lead):
    products = lax.dot_general(
        flipped, grads, (((0,), (0,)), ((), ())), preferred_element_type=jnp.float32
    )
    positions = products.shape[0]
    if keep is not None:
        products = jnp.where(keep, products, 0.0)
    if lead:
        products = jnp.concatenate([jnp.zeros((positions, lead), jnp.float32), products], axis=1)
    products = pltpu.roll(products, products.shape[1] - positions + 1, 1, stride=1, stride_axis=0)
    return jnp.sum(products, axis=0, keepdims=True)


def own_lags_kernel(place, own_input, peer_input, own_grad, peer_grad, out, flipped):
    first_core = place[0] == 0
    sequences, channels, positions = own_input.shape
    half = channels // CORES
    own_row = pl.multiple_of(place[0] * half, half)
    rows, width = sequences * GROUP_SIZE, CORES * positions
    flip = reversal(positions)
    row = lax.broadcasted_iota(jnp.int32, (positions, width), 0)
    column = lax.broadcasted_iota(jnp.int32, (positions, width), 1)
    keep = column + row >= positions - 1
    zeros = jnp.zeros((rows, positions), jnp.bfloat16)
    out[...] = jnp.zeros_like(out)

    def body(first, count):
        start = pl.multiple_of(own_row + first * GROUP_SIZE, GROUP_SIZE)
        own = own_input[:, pl.ds(start, count * GROUP_SIZE), :]
        peer = peer_input[:, pl.ds(start, count * GROUP_SIZE), :]
        flip_rows(flipped, 0, pick(first_core, own, peer), flip)
        flip_rows(flipped, 1, pick(first_core, peer, own), flip)
        for index in range(count):
            values = jnp.concatenate(
                [group_rows(flipped.at[core], index) for core in range(CORES)], axis=0
            )
            own = group_rows(own_grad, index, start)
            peer = group_rows(peer_grad, index, start)
            early, late = pick(first_core, own, peer), pick(first_core, peer, own)
            grads = jnp.concatenate(
                [jnp.concatenate([early, late], axis=1), jnp.concatenate([late, zeros], axis=1)], axis=0
            )
            out[pl.ds(first + index, 1), :width] = lag_sums(values, grads, keep, 0)

    chunked(half // GROUP_SIZE, body)


def round_lags_kernel(
    chips, distance, place, own_input, peer_input, own_grad, peer_grad, own_got, peer_got, running, out, flipped
):
    first_core = place[0] == 0
    lower = place[1] + distance < chips
    sequences, channels, positions = own_input.shape
    part = channels // CORES // 2
    rows = sequences * GROUP_SIZE
    flip = reversal(positions)
    part_row = pl.multiple_of((place[0] * 2 + jnp.where(lower, 0, 1)) * part, part)
    part_group = pl.multiple_of(jnp.where(lower, 0, part // GROUP_SIZE), part // GROUP_SIZE)
    if 2 * distance == chips:
        first_lag = (2 * distance - 2) * positions
    else:
        first_lag = pl.multiple_of(
            jnp.where(lower, 2 * distance - 2, 2 * (chips - distance) - 2) * positions, positions
        )
    zeros = jnp.zeros((rows, positions), jnp.bfloat16)
    out[...] = running[...]

    def body(first, count):
        start = pl.multiple_of(first * GROUP_SIZE, GROUP_SIZE)
        own_rows = pl.ds(pl.multiple_of(part_row + start, GROUP_SIZE), count * GROUP_SIZE)
        got_rows = pl.ds(start, count * GROUP_SIZE)
        own = pick(lower, own_input[:, own_rows, :], own_got[:, got_rows, :])
        peer = pick(lower, peer_input[:, own_rows, :], peer_got[:, got_rows, :])
        flip_rows(flipped, 0, pick(first_core, own, peer), flip)
        flip_rows(flipped, 1, pick(first_core, peer, own), flip)
        for index in range(count):
            got = group_rows(own_got, index, start), group_rows(peer_got, index, start)
            grads = (
                group_rows(own_grad, index, part_row + start),
                group_rows(peer_grad, index, part_row + start),
            )
            right = [pick(lower, b, a) for a, b in zip(grads, got)]
            values = jnp.concatenate(
                [group_rows(flipped.at[core], index) for core in range(CORES)], axis=0
            )
            early, late = pick(first_core, *right), pick(first_core, *right[::-1])
            pairs = jnp.concatenate(
                [
                    jnp.concatenate([zeros, early, late], axis=1),
                    jnp.concatenate([early, late, zeros], axis=1),
                ],
                axis=0,
            )
            where = (pl.ds(part_group + first + index, 1), pl.ds(first_lag, 2 * CORES * positions))
            out[where] = out[where] + lag_sums(values, pairs, None, positions)

    chunked(part // GROUP_SIZE, body, 2 * UNROLL)


def assemble_kernel(out_place, *refs):
    parts, out, sems = refs[:-2], refs[-2], refs[-1]
    half = out.shape[1] // CORES
    core = out_place[0]
    copies = []
    start = core * half
    for number, ref in enumerate(parts):
        if number == len(parts) // 2:
            start = (1 - core) * half
        rows = pl.ds(pl.multiple_of(start, GROUP_SIZE), ref.shape[1])
        copies.append(pltpu.make_async_copy(ref, out.at[:, rows, :], sems.at[number]))
        start = start + ref.shape[1]
    for copy in copies:
        copy.start()
    for copy in copies:
        copy.wait()


def parts_kernel(chips, slot_rows, inputs, output_grad, filters, *refs):
    count = CORES * (chips - 1)
    outs, stages, in_sems, out_sems = refs[:count], refs[count : 2 * count], refs[-2], refs[-1]
    sequences = inputs.shape[0]
    half = inputs.shape[1] // CORES
    part = half // 2
    groups = filters.shape[0] // CORES
    own_index = lax.axis_index("seq")
    chip, core = lax.div(own_index, CORES), lax.rem(own_index, CORES)

    def arrivals(source, start, target, number):
        rows = pl.ds(pl.multiple_of(start, GROUP_SIZE), part)
        for sequence in range(sequences):
            pltpu.make_async_copy(
                source.at[sequence, rows, :], target.at[sequence, pl.ds(0, part), :], in_sems.at[number]
            ).start()

    for number in range(count):
        distance, other = number // CORES + 1, number % CORES
        whose = core if other == 0 else 1 - core
        start = whose * half
        target = stages[number]
        for sequence in range(sequences):
            slot = sequence if slot_rows < groups else 0
            row = pl.multiple_of(whose * groups + slot * slot_rows, GROUP_SIZE)
            pltpu.make_async_copy(
                filters.at[pl.ds(row, slot_rows), :],
                target.at[sequence, pl.ds(part, slot_rows), :],
                in_sems.at[number],
            ).start()
        lax.cond(
            chip >= distance,
            lambda: arrivals(output_grad, start, target, number),
            lambda: arrivals(inputs, start + part, target, number),
        )
    for number in range(count):
        pltpu.make_async_copy(stages[number], stages[number], in_sems.at[number]).wait()
        for sequence in range(sequences):
            pltpu.make_async_copy(stages[number].at[sequence], outs[number].at[sequence], out_sems.at[number]).start()
    for number in range(count):
        pltpu.make_async_copy(stages[number], outs[number], out_sems.at[number]).wait()


def second_kernel(own_grad, peer_grad, *refs):
    outs, sems = refs[:-1], refs[-1]
    sequences = own_grad.shape[0]
    half = own_grad.shape[1] // CORES
    core = lax.rem(lax.axis_index("seq"), CORES)
    start = core * half + half // 2
    copies = []
    for out in outs:
        for number, ref in enumerate((own_grad, peer_grad)):
            copies.append(
                pltpu.make_async_copy(
                    ref.at[:, pl.ds(pl.multiple_of(start, GROUP_SIZE), out.shape[1]), :],
                    out.at[pl.ds(number * sequences, sequences)],
                    sems.at[len(copies)],
                )
            )
        start = start + out.shape[1]
    for copy in copies:
        copy.start()
    for copy in copies:
        copy.wait()


def per_device(inputs, output_grad, filters):
    sequences, channels, positions = inputs.shape
    shard_count = lax.axis_size("seq")
    chips = shard_count // CORES
    own_index = lax.axis_index("seq")
    chip, core = own_index // CORES, own_index % CORES
    place = jnp.stack([core, chip]).astype(jnp.int32)
    half = channels // CORES
    part = half // 2
    groups = half // GROUP_SIZE
    slot_rows = groups // 2 if sequences == 2 and groups % (2 * GROUP_SIZE) == 0 else groups
    length = shard_count * positions
    rows = sequences * GROUP_SIZE
    rounds = range(1, chips)

    def swap_cores(value):
        return lax.ppermute(value, "seq", [(i, i ^ 1) for i in range(shard_count)])

    def from_chip(value, distance, wrap, other=0):
        pairs = [
            (i, (i - distance * CORES) % shard_count ^ other)
            for i in range(shard_count)
            if wrap or i >= distance * CORES
        ]
        return lax.ppermute(value, "seq", pairs)

    in_hbm = pl.BlockSpec(memory_space=pltpu.HBM)
    params = pltpu.CompilerParams(vmem_limit_bytes=VMEM_BYTES)

    heights = [part + slot_rows] * (CORES * (chips - 1))
    outgoing = pl.pallas_call(
        functools.partial(parts_kernel, chips, slot_rows),
        in_specs=[in_hbm] * 3,
        out_specs=[in_hbm] * len(heights),
        out_shape=[jax.ShapeDtypeStruct((sequences, height, positions), inputs.dtype) for height in heights],
        scratch_shapes=[pltpu.VMEM((sequences, height, positions), inputs.dtype) for height in heights]
        + [pltpu.SemaphoreType.DMA((len(heights),))] * 2,
    )(inputs, output_grad, filters)

    to_swap = (filters, output_grad, inputs)
    filters_peer, grad_peer, input_peer = (swap_cores(value) for value in to_swap)
    first = {
        k: [from_chip(outgoing[CORES * (k - 1) + other], k, True, other) for other in range(CORES)]
        for k in rounds
    }

    in_smem, in_vmem = pl.BlockSpec(memory_space=pltpu.SMEM), pl.BlockSpec(memory_space=pltpu.VMEM)
    flip_scratch = pltpu.VMEM((CORES, sequences, 2 * UNROLL * GROUP_SIZE, positions), jnp.bfloat16)

    def vmem(value):
        return pltpu.with_memory_space_constraint(value, pltpu.VMEM)

    def cost(group_count, depth, width, arrays):
        return pl.CostEstimate(
            flops=max(1, int(2 * group_count * depth * positions * width)),
            bytes_accessed=max(1, int(arrays * group_count * rows * positions * 2)),
            transcendentals=0,
        )

    input_here, grad_here = vmem(inputs), vmem(output_grad)
    input_peer, grad_peer = vmem(input_peer), vmem(grad_peer)
    both = (input_here, input_peer, grad_here, grad_peer)
    part_groups = groups // 2
    early_groups = part_groups * EARLY // 32
    sizes = [early_groups, part_groups - early_groups]
    outgoing = pl.pallas_call(
        second_kernel,
        in_specs=[in_vmem] * 2,
        out_specs=[in_hbm] * len(sizes),
        out_shape=[
            jax.ShapeDtypeStruct((CORES * sequences, size * GROUP_SIZE, positions), inputs.dtype) for size in sizes
        ],
        scratch_shapes=[pltpu.SemaphoreType.DMA((CORES * len(sizes),))],
    )(grad_here, grad_peer)
    second = [{k: [from_chip(outgoing[0], k, False)] for k in rounds}]

    lags = pl.pallas_call(
        own_lags_kernel,
        in_specs=[in_smem] + [in_vmem] * 4,
        out_specs=in_vmem,
        out_shape=pltpu.VMEM((groups, length), jnp.float32),
        scratch_shapes=[flip_scratch],
        cost_estimate=cost(groups * OWN_WEIGHT, CORES * rows, CORES * positions, 4),
        compiler_params=params,
    )(place, *both)

    for k in rounds:
        lags = pl.pallas_call(
            functools.partial(round_lags_kernel, chips, k),
            in_specs=[in_smem] + [in_vmem] * 7,
            out_specs=in_vmem,
            out_shape=pltpu.VMEM((groups, length), jnp.float32),
            scratch_shapes=[flip_scratch],
            cost_estimate=cost(groups // 2, CORES * rows, 3 * positions, 6),
            compiler_params=params,
        )(place, *both, *[vmem(ref) for ref in first[k]], vmem(lags))

    for k in rounds:
        lags, second[0][k][0] = lax.optimization_barrier((lags, second[0][k][0]))

    def chip_lags(which):
        return lax.dynamic_slice_in_dim(lags, which * CORES * positions, CORES * positions, 1)

    sums = chip_lags(chip)
    for k in rounds:
        sums = sums + from_chip(chip_lags((chip - k) % chips), k, True)

    def input_part(which, offset, count, received):
        come = [ref for k in rounds for ref in first[k]]
        arrays = [ref for k in rounds for ref in received[k]]
        values = [filters, filters_peer, *come, grad_here, grad_peer, *arrays]
        return pl.pallas_call(
            functools.partial(input_grad_kernel, chips, which, offset, slot_rows),
            in_specs=[in_smem] + [in_vmem] * len(values),
            out_specs=[in_vmem] * 2,
            out_shape=[jax.ShapeDtypeStruct((sequences, count * GROUP_SIZE, positions), jnp.bfloat16)] * 2,
            scratch_shapes=[pltpu.VMEM((groups, length), jnp.float32)],
            cost_estimate=cost(count if which and offset else PART_WEIGHT, CORES * rows, length, 4 + len(arrays)),
            compiler_params=params,
        )(place, *[vmem(value) for value in values])

    second.append({k: [from_chip(outgoing[1], k, False)] for k in rounds})
    for k in rounds:
        second[1][k][0], second[0][k][0] = lax.optimization_barrier((second[1][k][0], second[0][k][0]))
    results = [
        input_part(0, 0, part_groups, first),
        input_part(1, 0, sizes[0], second[0]),
        input_part(1, sizes[0], sizes[1], second[1]),
    ]
    sums, _ = lax.optimization_barrier((sums, results[0][0]))
    mine = jnp.concatenate([result[0] for result in results], axis=1)
    got = jnp.concatenate([swap_cores(result[1]) for result in results], axis=1)
    input_grad = jnp.where(
        core == 0, jnp.concatenate([mine, got], axis=1), jnp.concatenate([got, mine], axis=1)
    )

    keep = lax.dynamic_slice_in_dim(sums, core * positions, positions, 1)
    got = swap_cores(lax.dynamic_slice_in_dim(sums, (1 - core) * positions, positions, 1))
    own = jnp.where(core == 0, jnp.concatenate([keep, got], axis=0), jnp.concatenate([got, keep], axis=0))
    copies = lax.axis_size("dp")
    terms = [own]
    for k in range(1, copies):
        terms.append(lax.ppermute(own, "dp", [(i, i ^ k) for i in range(copies)]))
    while len(terms) > 1:
        terms = [a + b for a, b in zip(terms[::2], terms[1::2])]
    filter_grad = terms[0]
    return (input_grad, filter_grad)


def solution(mesh):
    in_specs = (P("dp", "chan", "seq"), P("dp", "chan", "seq"), P("chan", "seq"))
    out_specs = (P("dp", "chan", "seq"), P("chan", "seq"))
    return jax.shard_map(
        per_device, mesh=mesh, in_specs=in_specs, out_specs=out_specs, check_vma=False
    )
```
